256 devices in a mesh: inst: 4 (over y), batch: 8 (over z), tensor: 8 (over x, core).
Axes of the slice: x: 4, y: 4, z: 8, core: 2. Of those that a mesh axis runs over, the one named last changes fastest.
Arguments:
- queries: bfloat16 [256, 8192], P(('inst', 'batch'), 'tensor'), may hold values from -100 to 100
- current_key_value: bfloat16 [256, 2048], P(('inst', 'batch'), 'tensor'), may hold values from -6 to 6
- key_value_pages: bfloat16 [2048, 128, 2048], P(('inst', 'batch'), None, 'tensor'), may hold values from -6 to 6
- transfer_pages: int32 [32, 32], P(('inst', 'batch')), may hold values from -1 to 63, as said below
- request_pages: int32 [256, 8], P(('inst', 'batch')), may hold values from 0 to 95, as said below
- lengths: int32 [256], P(('inst', 'batch')), may hold values from 512 to 1024, as said below
- request_adapter: int32 [256], P('inst'), may hold values from 0 to 7
- residual_input: bfloat16 [256, 8192], P(('inst', 'tensor'), 'batch'), may hold values from -3 to 3
- wo: bfloat16 [8192, 8192], P('tensor', 'batch'), may hold values from -0.0625 to 0.0625
- down_weight: bfloat16 [8192, 512], P('tensor'), may hold values from -0.0625 to 0.0625
- up_weight: bfloat16 [512, 8192], P(None, 'batch'), may hold values from -0.75 to 0.75
Outputs:
- mixed: bfloat16 [256, 8192], P(('inst', 'tensor'), 'batch')
The draws below stay inside these ranges and needn't reach their ends.
Inputs may be any that keep to these rules, and one draw needn't show every extreme that they name: `transfer_pages`: row s gives, for each device p of inst+batch in turn, 1 slots: a page of device s's pool that s sends to p, or -1 for an empty slot. The filled slots of one row name distinct pages and none is addressed to s itself; some row fills all 1 slots toward some device. `request_pages`: an entry e names a page as stated in the first step; an entry of 64 or more names a filled slot of the migration list. Every filled slot is named exactly once among the rows of the device it is sent to, at page positions below 4. `lengths`: some request holds 1024 tokens.
All inputs are finite; a program needn't handle non-finite values.
Results may differ from the reference program's by a relative error of at most 0.014.
Values may be sent and summed in bfloat16 or wider, within the bound.
No kernel may reach another device: no remote copies, remote signals or barrier semaphores. Data moves between devices by JAX's collectives and lax.ppermute only.
A program may use at most 64 MiB of HBM per device.

```python
import math
import jax
import jax.numpy as jnp
from jax import lax

MODEL_WIDTH = 8192
KV_HEADS = 8
HEAD_DIM = 128
GROUP = 8
ADAPTER_RANK = 64
ADAPTER_COUNT = 8
SLOTS = 8
PAGE = 128
PAGES = 8
CAP = 1
PEERS = 32
POOL = 64
ROWS = 256
LEN = 1024


def migration_plan(key):
    first, second, third = jax.random.split(jax.random.fold_in(key, 101), 3)
    appetite = jax.random.randint(first, (PEERS,), 1, 8)
    target = jnp.arange(PEERS * CAP) // CAP
    rolled = jax.random.randint(second, (PEERS, PEERS * CAP), 0, 8)
    filled = rolled < appetite[target][None, :]
    sender = jnp.arange(PEERS)[:, None]
    filled = filled & (sender != target[None, :])
    filled = filled.at[0, CAP:2 * CAP].set(True)
    orders = jax.vmap(lambda subkey: jax.random.permutation(subkey, POOL))(jax.random.split(third, PEERS))
    pages_sent = jnp.where(filled, orders[:, :PEERS * CAP], -1).astype(jnp.int32)
    return (filled, pages_sent)


def draw_transfer_pages(key, part):
    filled, pages_sent = migration_plan(key)
    return pages_sent


def draw_request_pages(key, part):
    filled, pages_sent = migration_plan(key)
    key = jax.random.fold_in(key, 7)
    base_pages = jax.vmap(lambda subkey: jax.random.permutation(subkey, POOL))(jax.random.split(key, PEERS)).astype(jnp.int32)
    arrived = filled.reshape(PEERS, PEERS, CAP).transpose(1, 0, 2).reshape(PEERS, PEERS * CAP)
    ranking = jnp.cumsum(arrived.astype(jnp.int32), axis=1) - 1
    entries = jnp.arange(SLOTS * PAGES)
    order_key = entries % PAGES * SLOTS + entries // PAGES
    hits = arrived[:, None, :] & (ranking[:, None, :] == order_key[None, :, None])
    landed = jnp.any(hits, axis=-1)
    which = jnp.sum(jnp.where(hits, jnp.arange(PEERS * CAP)[None, None, :], 0), axis=-1)
    table = jnp.where(landed, POOL + which, base_pages)
    return table.reshape(PEERS * SLOTS, PAGES).astype(jnp.int32)


def draw_lengths(key, part):
    key = jax.random.fold_in(key, 17)
    values = jax.random.randint(key, (ROWS,), PAGES // 2 * PAGE, LEN + 1)
    return values.at[0].set(LEN).astype(jnp.int32)


def draw_key_value_pages(key, part):
    key = jax.random.fold_in(key, 29)
    first, second = jax.random.split(key, 2)
    dims_all = (PEERS * POOL, PAGE, 2 * KV_HEADS * HEAD_DIM)
    dims_page = (PEERS * POOL, 1, 2 * KV_HEADS * HEAD_DIM)
    noise = jax.random.normal(first, dims_all, jnp.float32)
    offset = jax.random.normal(second, dims_page, jnp.float32)
    values = noise + 0.8 * offset
    return jnp.clip(values, -6.0, 6.0).astype(jnp.bfloat16)


def draw_queries(key, part):
    key = jax.random.fold_in(key, 13)
    first = jax.random.fold_in(key, 0)
    dims_all = (ROWS, KV_HEADS * GROUP, HEAD_DIM)
    values = jnp.clip(jax.random.normal(first, dims_all, jnp.float32), -6.0, 6.0)
    return values.reshape(ROWS, KV_HEADS * GROUP * HEAD_DIM).astype(jnp.bfloat16)


def plant(values, key, least, high):
    shape = values.shape
    place = [jax.random.randint(jax.random.fold_in(key, axis), (), 0, shape[axis]) for axis in range(len(shape))]
    values = values.at[tuple(place)].set(least)
    longest = shape.index(max(shape))
    place[longest] = (place[longest] + 1) % shape[longest]
    return values.at[tuple(place)].set(high)


def level_of(rng, shape, cuts, low, top_value):
    level = 1.0
    for axis_at, shards_of in cuts:
        heights = jax.random.uniform(jax.random.fold_in(jax.random.fold_in(rng, 6), axis_at), (shards_of,), jnp.float32, low / len(cuts), top_value / len(cuts))
        level = level * jnp.repeat(jnp.exp(heights), shape[axis_at] // shards_of).reshape((-1,) + (1,) * (len(shape) - 1 - axis_at))
    return level


def bell_draw(key, shape, deviation, limit, shards=(), held_as=jnp.bfloat16):
    values = jax.random.normal(key, shape, jnp.float32) * deviation
    if len(shards) > 0:
        values = level_of(key, shape, shards, -0.22, 0.18) * values
    return jnp.clip(values, min=-limit, max=limit).astype(held_as)


def setup_inputs(seed: int = 0) -> dict:
    key_list = jax.random.split(jax.random.key(seed), 12)
    queries = draw_queries(jax.random.fold_in(key_list[11], 71), 0)
    current_key_value = bell_draw(key_list[1], (ROWS, 2 * KV_HEADS * HEAD_DIM), 1.0, 6.0, ((0, 32), (1, 8)))
    key_value_pages = draw_key_value_pages(jax.random.fold_in(key_list[11], 71), 0)
    transfer_pages = draw_transfer_pages(jax.random.fold_in(key_list[11], 71), 0)
    request_pages = draw_request_pages(jax.random.fold_in(key_list[11], 71), 0)
    lengths = draw_lengths(jax.random.fold_in(key_list[11], 71), 0)
    request_adapter = plant(jax.random.randint(key_list[6], (ROWS,), 0, ADAPTER_COUNT), jax.random.fold_in(key_list[6], 1), 0, ADAPTER_COUNT - 1).astype(jnp.int32)
    residual_input = bell_draw(key_list[7], (ROWS, MODEL_WIDTH), 0.5, 3.0, ((0, 32), (1, 8)))
    wo = bell_draw(key_list[8], (MODEL_WIDTH, MODEL_WIDTH), MODEL_WIDTH ** -0.5, 0.0625, ((0, 8), (1, 8)))
    down_weight = bell_draw(key_list[9], (MODEL_WIDTH, ADAPTER_COUNT * ADAPTER_RANK), MODEL_WIDTH ** -0.5, 0.0625, ((0, 8),))
    up_weight = bell_draw(key_list[10], (ADAPTER_COUNT * ADAPTER_RANK, MODEL_WIDTH), ADAPTER_RANK ** -0.5, 0.75, ((1, 8),))
    return dict(queries=queries, current_key_value=current_key_value, key_value_pages=key_value_pages, transfer_pages=transfer_pages, request_pages=request_pages, lengths=lengths, request_adapter=request_adapter, residual_input=residual_input, wo=wo, down_weight=down_weight, up_weight=up_weight)


def page_terms(query_heads, pages, counts):
    keys_part = pages[..., 0, :]
    values_part = pages[..., 1, :]
    scores = jnp.einsum('nkgd,npskd->npkgs', query_heads, keys_part) / math.sqrt(HEAD_DIM)
    positions = jnp.arange(pages.shape[2], dtype=jnp.int32)
    live = (positions[None, None, :] < counts[:, :, None])[:, :, None, None, :]
    masked = jnp.where(live, scores, -1e+30)
    page_max = lax.optimization_barrier(jnp.max(masked, axis=-1))
    probs = jnp.where(live, jnp.exp(masked - page_max[..., None]), 0.0).astype(jnp.bfloat16)
    weights = probs.astype(jnp.float32)
    page_sum = lax.optimization_barrier(jnp.sum(weights, axis=-1))
    page_out = jnp.einsum('npkgs,npskd->npkgd', weights, values_part)
    return (page_max, page_sum, page_out)

def combine(page_max, page_sum, page_out, own_score, new_values):
    peak = jnp.maximum(lax.optimization_barrier(jnp.max(page_max, axis=1)), own_score)
    scales = jnp.exp(page_max - peak[:, None])
    self_weight = jnp.exp(own_score - peak)
    numer = lax.optimization_barrier(jnp.sum(scales[..., None] * page_out, axis=1)) + self_weight[..., None] * new_values[:, :, None, :]
    denom = lax.optimization_barrier(jnp.sum(scales * page_sum, axis=1)) + self_weight
    return numer / denom[..., None]

def reference(queries, current_key_value, key_value_pages, transfer_pages, request_pages, lengths, request_adapter, residual_input, wo, down_weight, up_weight):
    row_count = request_pages.shape[0]
    device = (jnp.arange(row_count, dtype=jnp.int32) // SLOTS)[:, None]
    remote = request_pages >= POOL
    page_index = jnp.where(remote, request_pages - POOL, 0)
    sender = page_index // CAP
    sent_page = transfer_pages[sender, device * CAP + page_index % CAP]
    global_page = jnp.where(remote, sender * POOL + sent_page, device * POOL + request_pages).astype(jnp.int32)
    counts = jnp.clip(lengths[:, None] - jnp.arange(PAGES, dtype=jnp.int32)[None, :] * PAGE, 0, PAGE)

    def one_device(inputs):
        query_rows, fresh_rows, page_rows, count_rows = inputs
        query_heads = query_rows.astype(jnp.float32).reshape(SLOTS, KV_HEADS, GROUP, HEAD_DIM)
        fresh_kv = fresh_rows.astype(jnp.float32).reshape(SLOTS, KV_HEADS, 2, HEAD_DIM)
        pages = key_value_pages[page_rows].astype(jnp.float32).reshape(SLOTS, PAGES, PAGE, KV_HEADS, 2, HEAD_DIM)
        page_max, page_sum, page_out = page_terms(query_heads, pages, count_rows)
        own_score = jnp.einsum('nkgd,nkd->nkg', query_heads, fresh_kv[:, :, 0]) / math.sqrt(HEAD_DIM)
        result = combine(page_max, page_sum, page_out, own_score, fresh_kv[:, :, 1])
        return result.reshape(SLOTS, MODEL_WIDTH).astype(jnp.bfloat16)
    attention_output = lax.map(one_device, (queries.reshape(PEERS, SLOTS, MODEL_WIDTH), current_key_value.reshape(PEERS, SLOTS, 2 * KV_HEADS * HEAD_DIM), global_page.reshape(PEERS, SLOTS, PAGES), counts.reshape(PEERS, SLOTS, PAGES))).reshape(row_count, MODEL_WIDTH)
    base_part = jnp.dot(attention_output, wo, preferred_element_type=jnp.float32)
    reduced_total = jnp.dot(attention_output, down_weight, preferred_element_type=jnp.float32)
    onehot = (request_adapter[:, None] == jnp.arange(ADAPTER_COUNT, dtype=jnp.int32)[None, :]).astype(jnp.float32)
    chosen = lax.optimization_barrier(jnp.sum(reduced_total.reshape(row_count, ADAPTER_COUNT, ADAPTER_RANK) * onehot[:, :, None], axis=1))
    spread_values = (onehot[:, :, None] * chosen[:, None, :]).reshape(row_count, ADAPTER_COUNT * ADAPTER_RANK)
    adapter_update = jnp.dot(spread_values, up_weight.astype(jnp.float32), precision=lax.Precision.HIGHEST)
    return (residual_input.astype(jnp.float32) + base_part + adapter_update).astype(jnp.bfloat16)
```

```python
import math

import jax
import jax.numpy as jnp
from jax import lax
from jax.sharding import PartitionSpec as P

HEAD_DIM = 128
GROUP = 8
ADAPTER_RANK = 64


def body(
    queries,
    current_key_value,
    key_value_pages,
    transfer_pages,
    request_pages,
    lengths,
    request_adapter,
    residual_input,
    wo,
    down_weight,
    up_weight,
):
    slots, pages_per = request_pages.shape
    pool, page_len, _ = key_value_pages.shape
    peers = transfer_pages.shape[1]
    scale = 1.0 / math.sqrt(HEAD_DIM)
    q = queries.reshape(slots, GROUP, HEAD_DIM)
    named = request_pages[None] == pool + jnp.arange(peers, dtype=jnp.int32)[:, None, None]
    picks = jnp.any(named, axis=2)
    out_q = jnp.dot(picks.astype(jnp.bfloat16), queries, preferred_element_type=jnp.float32)
    out_q = out_q.astype(jnp.bfloat16).reshape(peers, GROUP, HEAD_DIM)
    in_q = lax.all_to_all(out_q, ("inst", "batch"), 0, 0, tiled=True)
    mine = request_pages < pool
    chosen = key_value_pages[jnp.where(mine, request_pages, 0)]
    chosen = chosen.reshape(slots, pages_per * page_len, 2 * HEAD_DIM)
    live = jnp.arange(pages_per * page_len, dtype=jnp.int32)[None] < lengths[:, None]
    live = live & jnp.repeat(mine, page_len, axis=1)
    scores = jnp.einsum(
        "ngd,nsd->ngs", q, chosen[..., :HEAD_DIM], preferred_element_type=jnp.float32
    ) * scale
    own = jnp.einsum(
        "ngd,nd->ng", q, current_key_value[:, :HEAD_DIM], preferred_element_type=jnp.float32
    ) * scale
    scores = jnp.where(live[:, None], scores, -1e30)
    top = jnp.maximum(jnp.max(scores, axis=-1), own)
    probs = jnp.where(live[:, None], jnp.exp(scores - top[..., None]), 0.0).astype(jnp.bfloat16)
    self_weight = jnp.exp(own - top)
    total = jnp.sum(probs.astype(jnp.float32), axis=-1) + self_weight
    numer = jnp.einsum(
        "ngs,nsd->ngd", probs, chosen[..., HEAD_DIM:], preferred_element_type=jnp.float32
    ) + self_weight[..., None] * current_key_value[:, None, HEAD_DIM:].astype(jnp.float32)
    sent = key_value_pages[jnp.maximum(transfer_pages[0], 0)]
    far_scores = jnp.einsum(
        "pgd,psd->pgs", in_q, sent[..., :HEAD_DIM], preferred_element_type=jnp.float32
    ) * scale
    far_top = jnp.max(far_scores, axis=-1)
    far_probs = jnp.exp(far_scores - far_top[..., None]).astype(jnp.bfloat16)
    far_total = jnp.sum(far_probs.astype(jnp.float32), axis=-1)
    far_out = jnp.einsum(
        "pgs,psd->pgd", far_probs, sent[..., HEAD_DIM:], preferred_element_type=jnp.float32
    ) / far_total[..., None]
    stats = jnp.concatenate([far_top[:, None], far_total[:, None]], 1)
    back_out = lax.all_to_all(
        far_out.astype(jnp.bfloat16), ("inst", "batch"), 0, 0, tiled=True
    )
    back_stats = lax.all_to_all(stats, ("inst", "batch"), 0, 0, tiled=True)
    back_top = back_stats[:, 0]
    back_total = back_stats[:, 1]
    reach = jnp.where(picks.T[:, :, None], back_top[None], -1e30)
    peak = jnp.maximum(jnp.max(reach, axis=1), top)
    weights = jnp.where(
        picks.T[:, :, None], jnp.exp(reach - peak[:, None]) * back_total[None], 0.0
    )
    keep = jnp.exp(top - peak)
    denom = keep * total + jnp.sum(weights, axis=1)
    numer = keep[..., None] * numer + jnp.einsum(
        "nsg,sgd->ngd", weights, back_out.astype(jnp.float32), precision=lax.Precision.HIGHEST
    )
    attended = (numer / denom[..., None]).astype(jnp.bfloat16).reshape(slots, -1)
    copies = jnp.broadcast_to(attended[None], (lax.axis_size("batch"),) + attended.shape)
    rows = lax.all_to_all(copies, "batch", 0, 0, tiled=True).reshape(-1, attended.shape[1])
    base = jnp.dot(rows, wo, preferred_element_type=jnp.float32)
    shrink = jnp.dot(rows, down_weight, preferred_element_type=jnp.float32)
    adapter_of = jnp.arange(down_weight.shape[1], dtype=jnp.int32) // ADAPTER_RANK
    shrink = jnp.where(request_adapter[:, None] == adapter_of[None], shrink, 0.0)
    high = shrink.astype(jnp.bfloat16)
    low = (shrink - high.astype(jnp.float32)).astype(jnp.bfloat16)
    both = jnp.dot(
        jnp.concatenate([high, low], 0), up_weight, preferred_element_type=jnp.float32
    )
    count = rows.shape[0]
    part = (base + both[:count] + both[count:]).astype(jnp.bfloat16)
    parts = lax.all_to_all(
        part.reshape(lax.axis_size("tensor"), -1, part.shape[1]), "tensor", 0, 0, tiled=True
    )
    summed = jnp.sum(parts.astype(jnp.float32), axis=0)
    return (residual_input.astype(jnp.float32) + summed).astype(jnp.bfloat16)


def solution(mesh):
    return jax.shard_map(
        body,
        mesh=mesh,
        in_specs=(
            P(("inst", "batch"), "tensor"),
            P(("inst", "batch"), "tensor"),
            P(("inst", "batch"), None, "tensor"),
            P(("inst", "batch"), None),
            P(("inst", "batch"), None),
            P(("inst", "batch")),
            P("inst"),
            P(("inst", "tensor"), "batch"),
            P("tensor", "batch"),
            P("tensor", None),
            P(None, "batch"),
        ),
        out_specs=P(("inst", "tensor"), "batch"),
        check_vma=False,
    )
```

```python
import math

import jax
import jax.numpy as jnp
from jax import lax
from jax.experimental import pallas as pl
from jax.experimental.pallas import tpu as pltpu
from jax.sharding import PartitionSpec as P

HEAD_DIM = 128
GROUP = 8
ADAPTER_RANK = 64
FAR_POSITIONS = 4
SCALE = 1.0 / math.sqrt(HEAD_DIM)
NEVER = -1e30
VMEM = pl.BlockSpec(memory_space=pltpu.VMEM)
SMEM = pl.BlockSpec(memory_space=pltpu.SMEM)
NT = (((1,), (1,)), ((), ()))


def heads_of(q_ref, q_heads):
    q = q_ref[...].astype(jnp.float32)
    for head in range(GROUP):
        q_heads[:, head, :] = q[:, head * HEAD_DIM:(head + 1) * HEAD_DIM]


def outgoing_kernel(pages_ref, q_ref, out_ref, q_heads, rows):
    slots, pool, peers = q_ref.shape[0], 64, out_ref.shape[0]
    heads_of(q_ref, q_heads)
    rows[...] = jnp.zeros_like(rows)
    for slot in range(slots):
        for place in range(FAR_POSITIONS):
            entry = pages_ref[slot, place]
            rows[jnp.where(entry >= pool, entry - pool, peers)] = q_heads[slot]
    out_ref[...] = rows[:peers].astype(jnp.bfloat16)


def near_kernel(
    pages_ref, lengths_ref, q_ref, fresh_ref, pool_ref, out_ref, top_ref, total_ref, q_heads
):
    slots, places = pages_ref.shape
    pool, page_len, _ = pool_ref.shape
    heads_of(q_ref, q_heads)
    fresh = fresh_ref[...].astype(jnp.float32)
    lane = lax.broadcasted_iota(jnp.int32, (GROUP, page_len), 1)
    for slot in range(slots):
        q = q_heads[slot]
        q_half = q.astype(jnp.bfloat16)
        index, scores = [], []
        for place in range(places):
            entry = pages_ref[slot, place]
            limit = lengths_ref[slot] - place * page_len
            if place < FAR_POSITIONS:
                limit = jnp.where(entry < pool, limit, 0)
                entry = jnp.where(entry < pool, entry, 0)
            index.append(entry)
            score = lax.dot_general(
                q_half, pool_ref[entry, :, :HEAD_DIM], NT, preferred_element_type=jnp.float32
            )
            scores.append(jnp.where(lane < limit, score * SCALE, NEVER))
        own = jnp.sum(q * fresh[slot:slot + 1, :HEAD_DIM], axis=1, keepdims=True) * SCALE
        top = scores[0]
        for score in scores[1:]:
            top = jnp.maximum(top, score)
        top = jnp.maximum(jnp.max(top, axis=1, keepdims=True), own)
        own_weight = jnp.exp(own - top)
        summed = jnp.zeros((GROUP, page_len), jnp.float32)
        out = own_weight * fresh[slot:slot + 1, HEAD_DIM:]
        for place in range(places):
            probs = jnp.exp(scores[place] - top).astype(jnp.bfloat16)
            summed = summed + probs.astype(jnp.float32)
            out = out + jnp.dot(
                probs, pool_ref[index[place], :, HEAD_DIM:], preferred_element_type=jnp.float32
            )
        total = jnp.sum(summed, axis=1, keepdims=True) + own_weight
        out_ref[slot] = out
        top_ref[slot] = jnp.broadcast_to(top, (GROUP, HEAD_DIM))
        total_ref[slot] = jnp.broadcast_to(total, (GROUP, HEAD_DIM))


def far_kernel(listed_ref, q_ref, pool_ref, out_ref):
    peers = q_ref.shape[0]
    lane = lax.broadcasted_iota(jnp.int32, (GROUP, HEAD_DIM), 1)
    for peer in range(peers):
        page = jnp.maximum(listed_ref[0, peer], 0)
        score = SCALE * lax.dot_general(
            q_ref[peer], pool_ref[page, :, :HEAD_DIM], NT, preferred_element_type=jnp.float32
        )
        top = jnp.max(score, axis=1, keepdims=True).astype(jnp.bfloat16).astype(jnp.float32)
        probs = jnp.exp(score - top).astype(jnp.bfloat16)
        total = jnp.sum(probs.astype(jnp.float32), axis=1, keepdims=True)
        out = jnp.dot(probs, pool_ref[page, :, HEAD_DIM:], preferred_element_type=jnp.float32)
        high = total.astype(jnp.bfloat16).astype(jnp.float32)
        stats = jnp.where(lane == 0, top, jnp.where(lane == 1, high, total - high))
        out_ref[peer] = jnp.concatenate([out / total, stats], 0).astype(jnp.bfloat16)


def join_kernel(pages_ref, out_ref, top_ref, total_ref, back_ref, rows_ref, heads):
    slots, pool = pages_ref.shape[0], 64
    for slot in range(slots):
        tops, totals, outs = [top_ref[slot]], [total_ref[slot]], [out_ref[slot]]
        for place in range(FAR_POSITIONS):
            entry = pages_ref[slot, place]
            part = back_ref[jnp.maximum(entry - pool, 0)].astype(jnp.float32)
            stats = part[GROUP:]
            tops.append(jnp.where(entry >= pool, stats[:, 0:1], NEVER))
            totals.append(stats[:, 1:2] + stats[:, 2:3])
            outs.append(part[:GROUP])
        peak = tops[0]
        for top in tops[1:]:
            peak = jnp.maximum(peak, top)
        keep = jnp.exp(tops[0] - peak)
        denom = keep * totals[0]
        numer = keep * outs[0]
        for top, total, out in zip(tops[1:], totals[1:], outs[1:]):
            weight = jnp.exp(top - peak) * total
            denom = denom + weight
            numer = numer + weight * out
        heads[slot] = numer / denom
    for head in range(GROUP):
        block = heads[:, head, :].astype(jnp.bfloat16)
        for copy in range(rows_ref.shape[0]):
            rows_ref[copy, :, head * HEAD_DIM:(head + 1) * HEAD_DIM] = block


def body(
    queries,
    current_key_value,
    key_value_pages,
    transfer_pages,
    request_pages,
    lengths,
    request_adapter,
    residual_input,
    wo,
    down_weight,
    up_weight,
):
    slots, _ = request_pages.shape
    peers = transfer_pages.shape[1]
    heads = (slots, GROUP, HEAD_DIM)
    around = ("inst", "batch")
    params = pltpu.CompilerParams(vmem_limit_bytes=16 * 1024 * 1024)
    out_q = pl.pallas_call(
        outgoing_kernel,
        out_shape=jax.ShapeDtypeStruct((peers, GROUP, HEAD_DIM), jnp.bfloat16),
        in_specs=[SMEM, VMEM],
        out_specs=VMEM,
        scratch_shapes=[
            pltpu.VMEM(heads, jnp.float32),
            pltpu.VMEM((peers + 1, GROUP, HEAD_DIM), jnp.float32),
        ],
        compiler_params=params,
        name="outgoing",
    )(request_pages, queries)
    in_q = lax.all_to_all(out_q, around, 0, 0, tiled=True)
    near_out, near_top, near_total = pl.pallas_call(
        near_kernel,
        out_shape=[jax.ShapeDtypeStruct(heads, jnp.float32)] * 3,
        in_specs=[SMEM, SMEM, VMEM, VMEM, VMEM],
        out_specs=[VMEM] * 3,
        scratch_shapes=[pltpu.VMEM(heads, jnp.float32)],
        compiler_params=params,
        cost_estimate=pl.CostEstimate(flops=34_000_000, bytes_accessed=4_300_000, transcendentals=70_000),
        name="near",
    )(request_pages, lengths, queries, current_key_value, key_value_pages)
    far = pl.pallas_call(
        far_kernel,
        out_shape=jax.ShapeDtypeStruct((peers, 2 * GROUP, HEAD_DIM), jnp.bfloat16),
        in_specs=[SMEM, VMEM, VMEM],
        out_specs=VMEM,
        compiler_params=params,
        cost_estimate=pl.CostEstimate(flops=17_000_000, bytes_accessed=2_200_000, transcendentals=35_000),
        name="far",
    )(transfer_pages, in_q, key_value_pages)
    back = lax.all_to_all(far, around, 0, 0, tiled=True)
    group = lax.axis_size("batch")
    copies = pl.pallas_call(
        join_kernel,
        out_shape=jax.ShapeDtypeStruct((group, slots, GROUP * HEAD_DIM), jnp.bfloat16),
        in_specs=[SMEM, VMEM, VMEM, VMEM, VMEM],
        out_specs=VMEM,
        scratch_shapes=[pltpu.VMEM(heads, jnp.float32)],
        compiler_params=params,
        name="join",
    )(request_pages, near_out, near_top, near_total, back)
    rows = lax.all_to_all(copies, "batch", 0, 0, tiled=True).reshape(-1, GROUP * HEAD_DIM)
    base = jnp.dot(rows, wo, preferred_element_type=jnp.float32)
    shrink = jnp.dot(rows, down_weight, preferred_element_type=jnp.float32)
    adapter_of = jnp.arange(down_weight.shape[1], dtype=jnp.int32) // ADAPTER_RANK
    shrink = jnp.where(request_adapter[:, None] == adapter_of[None], shrink, 0.0)
    high = shrink.astype(jnp.bfloat16)
    low = (shrink - high.astype(jnp.float32)).astype(jnp.bfloat16)
    both = jnp.dot(
        jnp.concatenate([high, low], 0), up_weight, preferred_element_type=jnp.float32
    )
    count = rows.shape[0]
    part = (base + both[:count] + both[count:]).astype(jnp.bfloat16)
    parts = lax.all_to_all(
        part.reshape(lax.axis_size("tensor"), -1, part.shape[1]), "tensor", 0, 0, tiled=True
    )
    summed = jnp.sum(parts.astype(jnp.float32), axis=0)
    return (residual_input.astype(jnp.float32) + summed).astype(jnp.bfloat16)


def solution(mesh):
    return jax.shard_map(
        body,
        mesh=mesh,
        in_specs=(
            P(("inst", "batch"), "tensor"),
            P(("inst", "batch"), "tensor"),
            P(("inst", "batch"), None, "tensor"),
            P(("inst", "batch"), None),
            P(("inst", "batch"), None),
            P(("inst", "batch")),
            P("inst"),
            P(("inst", "tensor"), "batch"),
            P("tensor", "batch"),
            P("tensor", None),
            P(None, "batch"),
        ),
        out_specs=P(("inst", "tensor"), "batch"),
        check_vma=False,
    )
```

```python
import math

import jax
import jax.numpy as jnp
from jax import lax
from jax.experimental import pallas as pl
from jax.experimental.pallas import tpu as pltpu
from jax.sharding import PartitionSpec as P

HEAD_DIM = 128
GROUP = 8
ADAPTER_RANK = 64
FAR_POSITIONS = 4
FAR_BLOCK = 32
NEAR_BLOCK = 4
POOL = 64
SCALE = 1.0 / math.sqrt(HEAD_DIM)
NEVER = -1e30
VMEM = pl.BlockSpec(memory_space=pltpu.VMEM)
SMEM = pl.BlockSpec(memory_space=pltpu.SMEM)
HBM = pl.BlockSpec(memory_space=pltpu.HBM)
NT = (((1,), (1,)), ((), ()))


def in_hbm(array):
    return pltpu.with_memory_space_constraint(array, pltpu.HBM)


def heads_of(q_ref, q_heads):
    q = q_ref[...].astype(jnp.float32)
    for head in range(GROUP):
        q_heads[:, head, :] = q[:, head * HEAD_DIM:(head + 1) * HEAD_DIM]


def outgoing_kernel(
    pages_hbm, q_hbm, listed_hbm, out_ref, listed_ref, pages_ref, q_ref, q_heads, rows, sems
):
    first = pltpu.make_async_copy(q_hbm, q_ref, sems.at[0])
    second = pltpu.make_async_copy(pages_hbm, pages_ref, sems.at[1])
    third = pltpu.make_async_copy(listed_hbm, listed_ref, sems.at[2])
    first.start()
    second.start()
    third.start()
    rows[...] = jnp.zeros_like(rows)
    first.wait()
    heads_of(q_ref, q_heads)
    second.wait()
    slots, peers = q_ref.shape[0], out_ref.shape[0]
    for slot in range(slots):
        for place in range(FAR_POSITIONS):
            entry = pages_ref[slot, place]
            rows[jnp.where(entry >= POOL, entry - POOL, peers)] = q_heads[slot]
    out_ref[...] = rows[:peers].astype(jnp.bfloat16)
    third.wait()


def near_kernel(
    pages_ref, lengths_ref, adapter_ref, q_ref, fresh_ref, pool_ref,
    out_ref, top_ref, total_ref, which_ref, q_heads,
):
    slots, places = pages_ref.shape
    page_len = pool_ref.shape[1]
    heads_of(q_ref, q_heads)
    fresh = fresh_ref[...].astype(jnp.float32)
    lane = lax.broadcasted_iota(jnp.int32, (GROUP, page_len), 1)
    for first in range(0, slots, NEAR_BLOCK):
        block = range(first, first + NEAR_BLOCK)
        index = {}
        scores = {}
        for slot in block:
            limits = []
            for place in range(places):
                entry = pages_ref[slot, place]
                limit = lengths_ref[slot] - place * page_len
                if place < FAR_POSITIONS:
                    limit = jnp.where(entry < POOL, limit, 0)
                    entry = jnp.where(entry < POOL, entry, 0)
                index[slot, place] = entry
                limits.append(limit)
            keys = [pool_ref[index[slot, place], :, :HEAD_DIM] for place in range(places)]
            score = SCALE * lax.dot_general(
                q_heads[slot].astype(jnp.bfloat16),
                jnp.concatenate(keys, 0),
                NT,
                preferred_element_type=jnp.float32,
            )
            scores[slot] = [
                jnp.where(lane < limit, score[:, at * page_len:(at + 1) * page_len], NEVER)
                for at, limit in enumerate(limits)
            ]
        owns = [
            SCALE
            * jnp.sum(q_heads[slot] * fresh[slot:slot + 1, :HEAD_DIM], axis=1, keepdims=True)
            for slot in block
        ]
        tops = []
        for slot, own in zip(block, owns):
            top = scores[slot][0]
            for score in scores[slot][1:]:
                top = jnp.maximum(top, score)
            tops.append(jnp.maximum(jnp.max(top, axis=1, keepdims=True), own))
        weights = [jnp.exp(own - top) for own, top in zip(owns, tops)]
        for slot, top, weight in zip(block, tops, weights):
            probs = [jnp.exp(score - top).astype(jnp.bfloat16) for score in scores[slot]]
            summed = probs[0].astype(jnp.float32)
            for prob in probs[1:]:
                summed = summed + prob.astype(jnp.float32)
            values = [pool_ref[index[slot, place], :, HEAD_DIM:] for place in range(places)]
            out = jnp.dot(
                jnp.concatenate(probs, 1),
                jnp.concatenate(values, 0),
                preferred_element_type=jnp.float32,
            )
            total = jnp.sum(summed, axis=1, keepdims=True) + weight
            out_ref[slot] = out + weight * fresh[slot:slot + 1, HEAD_DIM:]
            top_ref[slot] = jnp.broadcast_to(top, (GROUP, HEAD_DIM))
            total_ref[slot] = jnp.broadcast_to(total, (GROUP, HEAD_DIM))
    for row in range(which_ref.shape[0]):
        which_ref[row:row + 1, :] = jnp.full((1, HEAD_DIM), adapter_ref[row], jnp.int32)


def far_kernel(listed_ref, q_ref, pool_ref, out_ref):
    peers = q_ref.shape[0]
    page_len = pool_ref.shape[1]
    lane = lax.broadcasted_iota(jnp.int32, (GROUP, HEAD_DIM), 1)
    none = jnp.zeros((GROUP, page_len), jnp.bfloat16)
    for first in range(0, peers, FAR_BLOCK):
        block = range(first, first + FAR_BLOCK)
        pages = [jnp.maximum(listed_ref[0, peer], 0) for peer in block]
        scores = []
        for at in range(0, FAR_BLOCK, 2):
            peer = first + at
            keys = jnp.concatenate(
                [pool_ref[pages[at], :, :HEAD_DIM], pool_ref[pages[at + 1], :, :HEAD_DIM]], 0
            )
            both = jnp.concatenate([q_ref[peer], q_ref[peer + 1]], 0)
            score = SCALE * lax.dot_general(both, keys, NT, preferred_element_type=jnp.float32)
            scores += [score[:GROUP, :page_len], score[GROUP:, page_len:]]
        tops = [
            jnp.max(score, axis=1, keepdims=True).astype(jnp.bfloat16).astype(jnp.float32)
            for score in scores
        ]
        probs = [jnp.exp(score - top).astype(jnp.bfloat16) for score, top in zip(scores, tops)]
        totals = [jnp.sum(prob.astype(jnp.float32), axis=1, keepdims=True) for prob in probs]
        outs = []
        for at in range(0, FAR_BLOCK, 2):
            values = jnp.concatenate(
                [pool_ref[pages[at], :, HEAD_DIM:], pool_ref[pages[at + 1], :, HEAD_DIM:]], 0
            )
            both = jnp.concatenate(
                [
                    jnp.concatenate([probs[at], none], 1),
                    jnp.concatenate([none, probs[at + 1]], 1),
                ],
                0,
            )
            out = jnp.dot(both, values, preferred_element_type=jnp.float32)
            outs += [out[:GROUP], out[GROUP:]]
        for peer, out, top, total in zip(block, outs, tops, totals):
            high = total.astype(jnp.bfloat16).astype(jnp.float32)
            stats = jnp.where(lane == 0, top, jnp.where(lane == 1, high, total - high))
            out_ref[peer] = jnp.concatenate([out / total, stats], 0).astype(jnp.bfloat16)


def join_kernel(pages_ref, out_ref, top_ref, total_ref, back_ref, rows_ref, heads):
    slots = range(pages_ref.shape[0])
    places = range(FAR_POSITIONS)
    entries = [[pages_ref[slot, place] for place in places] for slot in slots]
    parts = [
        [back_ref[jnp.maximum(entry - POOL, 0)].astype(jnp.float32) for entry in row]
        for row in entries
    ]
    tops = [
        [jnp.where(entry >= POOL, part[GROUP:, 0:1], NEVER) for entry, part in zip(*pair)]
        for pair in zip(entries, parts)
    ]
    totals = [[part[GROUP:, 1:2] + part[GROUP:, 2:3] for part in row] for row in parts]
    near_tops = [top_ref[slot] for slot in slots]
    peaks = near_tops
    for place in places:
        peaks = [jnp.maximum(peak, row[place]) for peak, row in zip(peaks, tops)]
    keeps = [jnp.exp(top - peak) for top, peak in zip(near_tops, peaks)]
    denoms = [keep * total_ref[slot] for slot, keep in zip(slots, keeps)]
    numers = [keep * out_ref[slot] for slot, keep in zip(slots, keeps)]
    for place in places:
        for slot in slots:
            weight = jnp.exp(tops[slot][place] - peaks[slot]) * totals[slot][place]
            denoms[slot] = denoms[slot] + weight
            numers[slot] = numers[slot] + weight * parts[slot][place][:GROUP]
    for slot in slots:
        heads[slot] = numers[slot] / denoms[slot]
    for head in range(GROUP):
        block = heads[:, head, :].astype(jnp.bfloat16)
        for copy in range(rows_ref.shape[0]):
            rows_ref[copy, :, head * HEAD_DIM:(head + 1) * HEAD_DIM] = block


def project_kernel(rows_ref, which_ref, wo_ref, down_ref, up_ref, part_ref):
    rows = rows_ref[...]
    count = rows.shape[0]
    shrink = jnp.dot(rows, down_ref[...], preferred_element_type=jnp.float32)
    base = jnp.dot(rows, wo_ref[...], preferred_element_type=jnp.float32)
    adapter_of = lax.broadcasted_iota(jnp.int32, shrink.shape, 1) // ADAPTER_RANK
    which = jnp.concatenate([which_ref[...]] * (shrink.shape[1] // which_ref.shape[1]), 1)
    shrink = jnp.where(which == adapter_of, shrink, 0.0)
    high = shrink.astype(jnp.bfloat16)
    low = (shrink - high.astype(jnp.float32)).astype(jnp.bfloat16)
    both = jnp.dot(
        jnp.concatenate([high, low], 0), up_ref[...], preferred_element_type=jnp.float32
    )
    part_ref[...] = (base + both[:count] + both[count:]).astype(jnp.bfloat16)


def body(
    queries,
    current_key_value,
    key_value_pages,
    transfer_pages,
    request_pages,
    lengths,
    request_adapter,
    residual_input,
    wo,
    down_weight,
    up_weight,
):
    slots, _ = request_pages.shape
    peers = transfer_pages.shape[1]
    heads = (slots, GROUP, HEAD_DIM)
    around = ("inst", "batch")
    params = pltpu.CompilerParams(vmem_limit_bytes=16 * 1024 * 1024)
    out_q, listed = pl.pallas_call(
        outgoing_kernel,
        out_shape=[
            jax.ShapeDtypeStruct((peers, GROUP, HEAD_DIM), jnp.bfloat16),
            jax.ShapeDtypeStruct(transfer_pages.shape, jnp.int32),
        ],
        in_specs=[HBM, HBM, HBM],
        out_specs=[VMEM, VMEM],
        scratch_shapes=[
            pltpu.SMEM(request_pages.shape, jnp.int32),
            pltpu.VMEM(queries.shape, jnp.bfloat16),
            pltpu.VMEM(heads, jnp.float32),
            pltpu.VMEM((peers + 1, GROUP, HEAD_DIM), jnp.float32),
            pltpu.SemaphoreType.DMA((3,)),
        ],
        compiler_params=params,
        cost_estimate=pl.CostEstimate(
            flops=100_000_000_000, bytes_accessed=400_000_000, transcendentals=0
        ),
        name="outgoing",
    )(in_hbm(request_pages), in_hbm(queries), in_hbm(transfer_pages))
    in_q = lax.all_to_all(out_q, around, 0, 0, tiled=True)
    near_out, near_top, near_total, which = pl.pallas_call(
        near_kernel,
        out_shape=[jax.ShapeDtypeStruct(heads, jnp.float32)] * 3
        + [jax.ShapeDtypeStruct((request_adapter.shape[0], HEAD_DIM), jnp.int32)],
        in_specs=[SMEM, SMEM, SMEM, VMEM, VMEM, VMEM],
        out_specs=[VMEM] * 4,
        scratch_shapes=[pltpu.VMEM(heads, jnp.float32)],
        compiler_params=params,
        cost_estimate=pl.CostEstimate(
            flops=34_000_000, bytes_accessed=14_000_000, transcendentals=70_000
        ),
        name="near",
    )(request_pages, lengths, request_adapter, queries, current_key_value, key_value_pages)
    far = pl.pallas_call(
        far_kernel,
        out_shape=jax.ShapeDtypeStruct((peers, 2 * GROUP, HEAD_DIM), jnp.bfloat16),
        in_specs=[SMEM, VMEM, VMEM],
        out_specs=VMEM,
        compiler_params=params,
        cost_estimate=pl.CostEstimate(
            flops=17_000_000, bytes_accessed=4_200_000, transcendentals=35_000
        ),
        name="far",
    )(listed, in_q, key_value_pages)
    back = lax.all_to_all(far, around, 0, 0, tiled=True)
    group = lax.axis_size("batch")
    copies = pl.pallas_call(
        join_kernel,
        out_shape=jax.ShapeDtypeStruct((group, slots, GROUP * HEAD_DIM), jnp.bfloat16),
        in_specs=[SMEM, VMEM, VMEM, VMEM, VMEM],
        out_specs=VMEM,
        scratch_shapes=[pltpu.VMEM(heads, jnp.float32)],
        compiler_params=params,
        cost_estimate=pl.CostEstimate(
            flops=100_000_000_000, bytes_accessed=400_000_000, transcendentals=0
        ),
        name="join",
    )(request_pages, near_out, near_top, near_total, back)
    rows = lax.all_to_all(copies, "batch", 0, 0, tiled=True).reshape(-1, GROUP * HEAD_DIM)
    part = pl.pallas_call(
        project_kernel,
        out_shape=jax.ShapeDtypeStruct((rows.shape[0], wo.shape[1]), jnp.bfloat16),
        in_specs=[VMEM] * 5,
        out_specs=VMEM,
        compiler_params=params,
        name="project",
    )(rows, which, wo, down_weight, up_weight)
    parts = lax.all_to_all(
        part.reshape(lax.axis_size("tensor"), -1, part.shape[1]), "tensor", 0, 0, tiled=True
    )
    summed = jnp.sum(parts.astype(jnp.float32), axis=0)
    return (residual_input.astype(jnp.float32) + summed).astype(jnp.bfloat16)


def solution(mesh):
    return jax.shard_map(
        body,
        mesh=mesh,
        in_specs=(
            P(("inst", "batch"), "tensor"),
            P(("inst", "batch"), "tensor"),
            P(("inst", "batch"), None, "tensor"),
            P(("inst", "batch"), None),
            P(("inst", "batch"), None),
            P(("inst", "batch")),
            P("inst"),
            P(("inst", "tensor"), "batch"),
            P("tensor", "batch"),
            P("tensor", None),
            P(None, "batch"),
        ),
        out_specs=P(("inst", "tensor"), "batch"),
        check_vma=False,
    )
```

```python
import math

import jax
import jax.numpy as jnp
from jax import lax
from jax.experimental import pallas as pl
from jax.experimental.pallas import tpu as pltpu
from jax.sharding import PartitionSpec as P

HEAD_DIM = 128
GROUP = 8
ADAPTER_RANK = 64
FAR_POSITIONS = 4
FAR_BLOCK = 32
NEAR_BLOCK = 4
POOL = 64
SCALE = 1.0 / math.sqrt(HEAD_DIM)
NEVER = -1e30
VMEM = pl.BlockSpec(memory_space=pltpu.VMEM)
HBM = pl.BlockSpec(memory_space=pltpu.HBM)
NT = (((1,), (1,)), ((), ()))


def in_hbm(array):
    return pltpu.with_memory_space_constraint(array, pltpu.HBM)


def down_rows(line):
    square = (line.shape[1], line.shape[1])
    diagonal = lax.broadcasted_iota(jnp.int32, square, 0) == lax.broadcasted_iota(
        jnp.int32, square, 1
    )
    column = jnp.sum(jnp.where(diagonal, line.astype(jnp.float32), 0.0), axis=1, keepdims=True)
    return column.astype(jnp.int32)


def heads_of(q_ref, q_heads):
    q = q_ref[...].astype(jnp.float32)
    for head in range(GROUP):
        q_heads[:, head, :] = q[:, head * HEAD_DIM:(head + 1) * HEAD_DIM]


def outgoing_kernel(pages_hbm, q_hbm, out_ref, pages_ref, q_ref, q_heads, rows, sems):
    first = pltpu.make_async_copy(q_hbm, q_ref, sems.at[0])
    second = pltpu.make_async_copy(pages_hbm, pages_ref, sems.at[1])
    first.start()
    second.start()
    rows[...] = jnp.zeros_like(rows)
    first.wait()
    second.wait()
    heads_of(q_ref, q_heads)
    slots, peers = q_ref.shape[0], out_ref.shape[0]
    pages = pages_ref[...]
    targets = jnp.where(pages >= POOL, pages - POOL, peers)
    for slot in range(slots):
        for place in range(FAR_POSITIONS):
            rows[targets[slot, place]] = q_heads[slot]
    out_ref[...] = rows[:peers].astype(jnp.bfloat16)


def far_kernel(listed_ref, q_ref, pool_ref, out_ref):
    peers = q_ref.shape[0]
    page_len = pool_ref.shape[1]
    lane = lax.broadcasted_iota(jnp.int32, (GROUP, HEAD_DIM), 1)
    none = jnp.zeros((GROUP, page_len), jnp.bfloat16)
    listed = jnp.maximum(listed_ref[...], 0)
    for first in range(0, peers, FAR_BLOCK):
        block = range(first, first + FAR_BLOCK)
        pages = [listed[0, peer] for peer in block]
        scores = []
        for at in range(0, FAR_BLOCK, 2):
            peer = first + at
            keys = jnp.concatenate(
                [pool_ref[pages[at], :, :HEAD_DIM], pool_ref[pages[at + 1], :, :HEAD_DIM]], 0
            )
            both = jnp.concatenate([q_ref[peer], q_ref[peer + 1]], 0)
            score = SCALE * lax.dot_general(both, keys, NT, preferred_element_type=jnp.float32)
            scores += [score[:GROUP, :page_len], score[GROUP:, page_len:]]
        tops = [
            jnp.max(score, axis=1, keepdims=True).astype(jnp.bfloat16).astype(jnp.float32)
            for score in scores
        ]
        probs = [jnp.exp(score - top).astype(jnp.bfloat16) for score, top in zip(scores, tops)]
        totals = [jnp.sum(prob.astype(jnp.float32), axis=1, keepdims=True) for prob in probs]
        outs = []
        for at in range(0, FAR_BLOCK, 2):
            values = jnp.concatenate(
                [pool_ref[pages[at], :, HEAD_DIM:], pool_ref[pages[at + 1], :, HEAD_DIM:]], 0
            )
            both = jnp.concatenate(
                [
                    jnp.concatenate([probs[at], none], 1),
                    jnp.concatenate([none, probs[at + 1]], 1),
                ],
                0,
            )
            out = jnp.dot(both, values, preferred_element_type=jnp.float32)
            outs += [out[:GROUP], out[GROUP:]]
        for peer, out, top, total in zip(block, outs, tops, totals):
            high = total.astype(jnp.bfloat16).astype(jnp.float32)
            stats = jnp.where(lane == 0, top, jnp.where(lane == 1, high, total - high))
            out_ref[peer] = jnp.concatenate([out / total, stats], 0).astype(jnp.bfloat16)


def near_parts(pages_ref, lengths_ref, q_ref, fresh_ref, pool_ref, q_heads):
    slots, places = pages_ref.shape
    page_len = pool_ref.shape[1]
    pages = pages_ref[...]
    before = page_len * lax.broadcasted_iota(jnp.int32, pages.shape, 1)
    limits = jnp.where(pages < POOL, down_rows(lengths_ref[...]) - before, 0)
    pages = jnp.where(pages < POOL, pages, 0)
    heads_of(q_ref, q_heads)
    fresh = fresh_ref[...].astype(jnp.float32)
    lane = lax.broadcasted_iota(jnp.int32, (GROUP, page_len), 1)
    near_tops, near_totals, near_outs = [], [], []
    for first in range(0, slots, NEAR_BLOCK):
        block = range(first, first + NEAR_BLOCK)
        index = {}
        scores = {}
        for slot in block:
            for place in range(places):
                index[slot, place] = pages[slot, place]
            keys = [pool_ref[index[slot, place], :, :HEAD_DIM] for place in range(places)]
            score = SCALE * lax.dot_general(
                q_heads[slot].astype(jnp.bfloat16),
                jnp.concatenate(keys, 0),
                NT,
                preferred_element_type=jnp.float32,
            )
            scores[slot] = [
                jnp.where(
                    lane < limits[slot:slot + 1, at:at + 1],
                    score[:, at * page_len:(at + 1) * page_len],
                    NEVER,
                )
                for at in range(places)
            ]
        owns = [
            SCALE
            * jnp.sum(q_heads[slot] * fresh[slot:slot + 1, :HEAD_DIM], axis=1, keepdims=True)
            for slot in block
        ]
        tops = []
        for slot, own in zip(block, owns):
            top = scores[slot][0]
            for score in scores[slot][1:]:
                top = jnp.maximum(top, score)
            tops.append(jnp.maximum(jnp.max(top, axis=1, keepdims=True), own))
        weights = [jnp.exp(own - top) for own, top in zip(owns, tops)]
        for slot, top, weight in zip(block, tops, weights):
            probs = [jnp.exp(score - top).astype(jnp.bfloat16) for score in scores[slot]]
            summed = probs[0].astype(jnp.float32)
            for prob in probs[1:]:
                summed = summed + prob.astype(jnp.float32)
            values = [pool_ref[index[slot, place], :, HEAD_DIM:] for place in range(places)]
            out = jnp.dot(
                jnp.concatenate(probs, 1),
                jnp.concatenate(values, 0),
                preferred_element_type=jnp.float32,
            )
            total = jnp.sum(summed, axis=1, keepdims=True) + weight
            near_tops.append(top)
            near_totals.append(total)
            near_outs.append(out + weight * fresh[slot:slot + 1, HEAD_DIM:])
    return near_tops, near_totals, near_outs


def join_kernel(
    pages_ref, lengths_ref, q_ref, fresh_ref, pool_ref, back_ref, rows_ref, q_heads, heads
):
    near_tops, near_totals, near_outs = near_parts(
        pages_ref, lengths_ref, q_ref, fresh_ref, pool_ref, q_heads
    )
    slots = range(pages_ref.shape[0])
    places = range(FAR_POSITIONS)
    pages = pages_ref[...]
    senders = jnp.maximum(pages - POOL, 0)
    parts = [
        [back_ref[senders[slot, place]].astype(jnp.float32) for place in places]
        for slot in slots
    ]
    tops = [
        [
            jnp.where(
                pages[slot:slot + 1, place:place + 1] >= POOL,
                parts[slot][place][GROUP:, 0:1],
                NEVER,
            )
            for place in places
        ]
        for slot in slots
    ]
    totals = [[part[GROUP:, 1:2] + part[GROUP:, 2:3] for part in row] for row in parts]
    peaks = near_tops
    for place in places:
        peaks = [jnp.maximum(peak, row[place]) for peak, row in zip(peaks, tops)]
    keeps = [jnp.exp(top - peak) for top, peak in zip(near_tops, peaks)]
    denoms = [keep * total for total, keep in zip(near_totals, keeps)]
    numers = [keep * out for out, keep in zip(near_outs, keeps)]
    for place in places:
        for slot in slots:
            weight = jnp.exp(tops[slot][place] - peaks[slot]) * totals[slot][place]
            denoms[slot] = denoms[slot] + weight
            numers[slot] = numers[slot] + weight * parts[slot][place][:GROUP]
    for slot in slots:
        heads[slot] = numers[slot] / denoms[slot]
    for head in range(GROUP):
        block = heads[:, head, :].astype(jnp.bfloat16)
        for copy in range(rows_ref.shape[0]):
            rows_ref[copy, :, head * HEAD_DIM:(head + 1) * HEAD_DIM] = block


def project_kernel(rows_ref, which_ref, wo_ref, down_ref, up_ref, part_ref):
    rows = rows_ref[...]
    count = rows.shape[0]
    shrink = jnp.dot(rows, down_ref[...], preferred_element_type=jnp.float32)
    base = jnp.dot(rows, wo_ref[...], preferred_element_type=jnp.float32)
    adapter_of = lax.broadcasted_iota(jnp.int32, shrink.shape, 1) // ADAPTER_RANK
    which = down_rows(which_ref[...])
    shrink = jnp.where(which == adapter_of, shrink, 0.0)
    high = shrink.astype(jnp.bfloat16)
    low = (shrink - high.astype(jnp.float32)).astype(jnp.bfloat16)
    both = jnp.dot(
        jnp.concatenate([high, low], 0), up_ref[...], preferred_element_type=jnp.float32
    )
    part_ref[...] = (base + both[:count] + both[count:]).astype(jnp.bfloat16)


def body(
    queries,
    current_key_value,
    key_value_pages,
    transfer_pages,
    request_pages,
    lengths,
    request_adapter,
    residual_input,
    wo,
    down_weight,
    up_weight,
):
    slots, _ = request_pages.shape
    peers = transfer_pages.shape[1]
    heads = (slots, GROUP, HEAD_DIM)
    around = ("inst", "batch")
    params = pltpu.CompilerParams(vmem_limit_bytes=16 * 1024 * 1024)
    out_q = pl.pallas_call(
        outgoing_kernel,
        out_shape=jax.ShapeDtypeStruct((peers, GROUP, HEAD_DIM), jnp.bfloat16),
        in_specs=[HBM, HBM],
        out_specs=VMEM,
        scratch_shapes=[
            pltpu.VMEM(request_pages.shape, jnp.int32),
            pltpu.VMEM(queries.shape, jnp.bfloat16),
            pltpu.VMEM(heads, jnp.float32),
            pltpu.VMEM((peers + 1, GROUP, HEAD_DIM), jnp.float32),
            pltpu.SemaphoreType.DMA((2,)),
        ],
        compiler_params=params,
        cost_estimate=pl.CostEstimate(
            flops=100_000_000_000, bytes_accessed=400_000_000, transcendentals=0
        ),
        name="outgoing",
    )(in_hbm(request_pages), in_hbm(queries))
    in_q = lax.all_to_all(out_q, around, 0, 0, tiled=True)
    far = pl.pallas_call(
        far_kernel,
        out_shape=jax.ShapeDtypeStruct((peers, 2 * GROUP, HEAD_DIM), jnp.bfloat16),
        in_specs=[VMEM, VMEM, VMEM],
        out_specs=VMEM,
        compiler_params=params,
        cost_estimate=pl.CostEstimate(
            flops=100_000_000_000, bytes_accessed=400_000_000, transcendentals=0
        ),
        name="far",
    )(transfer_pages, in_q, key_value_pages)
    back = lax.all_to_all(far, around, 0, 0, tiled=True)
    group = lax.axis_size("batch")
    copies = pl.pallas_call(
        join_kernel,
        out_shape=jax.ShapeDtypeStruct((group, slots, GROUP * HEAD_DIM), jnp.bfloat16),
        in_specs=[VMEM] * 6,
        out_specs=VMEM,
        scratch_shapes=[pltpu.VMEM(heads, jnp.float32), pltpu.VMEM(heads, jnp.float32)],
        compiler_params=params,
        cost_estimate=pl.CostEstimate(
            flops=100_000_000_000, bytes_accessed=400_000_000, transcendentals=0
        ),
        name="join",
    )(
        request_pages,
        lengths[None],
        queries,
        current_key_value,
        key_value_pages,
        back,
    )
    rows = lax.all_to_all(copies, "batch", 0, 0, tiled=True).reshape(-1, GROUP * HEAD_DIM)
    part = pl.pallas_call(
        project_kernel,
        out_shape=jax.ShapeDtypeStruct((rows.shape[0], wo.shape[1]), jnp.bfloat16),
        in_specs=[VMEM] * 5,
        out_specs=VMEM,
        compiler_params=params,
        name="project",
    )(rows, request_adapter[None], wo, down_weight, up_weight)
    parts = lax.all_to_all(
        part.reshape(lax.axis_size("tensor"), -1, part.shape[1]), "tensor", 0, 0, tiled=True
    )
    summed = jnp.sum(parts.astype(jnp.float32), axis=0)
    return (residual_input.astype(jnp.float32) + summed).astype(jnp.bfloat16)


def solution(mesh):
    return jax.shard_map(
        body,
        mesh=mesh,
        in_specs=(
            P(("inst", "batch"), "tensor"),
            P(("inst", "batch"), "tensor"),
            P(("inst", "batch"), None, "tensor"),
            P(("inst", "batch"), None),
            P(("inst", "batch"), None),
            P(("inst", "batch")),
            P("inst"),
            P(("inst", "tensor"), "batch"),
            P("tensor", "batch"),
            P("tensor", None),
            P(None, "batch"),
        ),
        out_specs=P(("inst", "tensor"), "batch"),
        check_vma=False,
    )
```

```python
import math

import jax
import jax.numpy as jnp
from jax import lax
from jax.experimental import pallas as pl
from jax.experimental.pallas import tpu as pltpu
from jax.sharding import PartitionSpec as P

HEAD_DIM = 128
GROUP = 8
ADAPTER_RANK = 64
FAR_POSITIONS = 4
FAR_BLOCK = 32
NEAR_BLOCK = 8
POOL = 64
SCALE = 1.0 / math.sqrt(HEAD_DIM)
NEVER = -1e30
VMEM = pl.BlockSpec(memory_space=pltpu.VMEM)
HBM = pl.BlockSpec(memory_space=pltpu.HBM)
NT = (((1,), (1,)), ((), ()))


def in_hbm(array):
    return pltpu.with_memory_space_constraint(array, pltpu.HBM)


def down_rows(line):
    square = (line.shape[1], line.shape[1])
    diagonal = lax.broadcasted_iota(jnp.int32, square, 0) == lax.broadcasted_iota(
        jnp.int32, square, 1
    )
    column = jnp.sum(jnp.where(diagonal, line.astype(jnp.float32), 0.0), axis=1, keepdims=True)
    return column.astype(jnp.int32)


def heads_of(q_ref, q_heads):
    q = q_ref[...].astype(jnp.float32)
    for head in range(GROUP):
        q_heads[:, head, :] = q[:, head * HEAD_DIM:(head + 1) * HEAD_DIM]


def outgoing_kernel(pages_hbm, q_hbm, out_ref, pages_ref, q_ref, q_heads, rows, sems):
    first = pltpu.make_async_copy(q_hbm, q_ref, sems.at[0])
    second = pltpu.make_async_copy(pages_hbm, pages_ref, sems.at[1])
    first.start()
    second.start()
    rows[...] = jnp.zeros_like(rows)
    first.wait()
    second.wait()
    heads_of(q_ref, q_heads)
    slots, peers = q_ref.shape[0], out_ref.shape[0]
    pages = pages_ref[...]
    targets = jnp.where(pages >= POOL, pages - POOL, peers)
    for slot in range(slots):
        for place in range(FAR_POSITIONS):
            rows[targets[slot, place]] = q_heads[slot]
    out_ref[...] = rows[:peers].astype(jnp.bfloat16)


def far_kernel(listed_ref, q_ref, pool_ref, out_ref):
    peers = q_ref.shape[0]
    page_len = pool_ref.shape[1]
    lane = lax.broadcasted_iota(jnp.int32, (GROUP, HEAD_DIM), 1)
    none = jnp.zeros((GROUP, page_len), jnp.bfloat16)
    listed = jnp.maximum(listed_ref[...], 0)
    for first in range(0, peers, FAR_BLOCK):
        block = range(first, first + FAR_BLOCK)
        pages = [listed[0, peer] for peer in block]
        scores = []
        for at in range(0, FAR_BLOCK, 2):
            peer = first + at
            keys = jnp.concatenate(
                [pool_ref[pages[at], :, :HEAD_DIM], pool_ref[pages[at + 1], :, :HEAD_DIM]], 0
            )
            both = jnp.concatenate([q_ref[peer], q_ref[peer + 1]], 0)
            score = SCALE * lax.dot_general(both, keys, NT, preferred_element_type=jnp.float32)
            scores += [score[:GROUP, :page_len], score[GROUP:, page_len:]]
        tops = [
            jnp.max(score, axis=1, keepdims=True).astype(jnp.bfloat16).astype(jnp.float32)
            for score in scores
        ]
        probs = [jnp.exp(score - top).astype(jnp.bfloat16) for score, top in zip(scores, tops)]
        totals = [jnp.sum(prob.astype(jnp.float32), axis=1, keepdims=True) for prob in probs]
        outs = []
        for at in range(0, FAR_BLOCK, 2):
            values = jnp.concatenate(
                [pool_ref[pages[at], :, HEAD_DIM:], pool_ref[pages[at + 1], :, HEAD_DIM:]], 0
            )
            both = jnp.concatenate(
                [
                    jnp.concatenate([probs[at], none], 1),
                    jnp.concatenate([none, probs[at + 1]], 1),
                ],
                0,
            )
            out = jnp.dot(both, values, preferred_element_type=jnp.float32)
            outs += [out[:GROUP], out[GROUP:]]
        for peer, out, top, total in zip(block, outs, tops, totals):
            high = total.astype(jnp.bfloat16).astype(jnp.float32)
            stats = jnp.where(lane == 0, top, jnp.where(lane == 1, high, total - high))
            out_ref[peer] = jnp.concatenate([out / total, stats], 0).astype(jnp.bfloat16)


def near_parts(pages_ref, lengths_ref, q_ref, fresh_ref, pool_ref, q_heads):
    slots, places = pages_ref.shape
    page_len = pool_ref.shape[1]
    pages = pages_ref[...]
    before = page_len * lax.broadcasted_iota(jnp.int32, pages.shape, 1)
    limits = jnp.where(pages < POOL, down_rows(lengths_ref[...]) - before, 0)
    pages = jnp.where(pages < POOL, pages, 0)
    heads_of(q_ref, q_heads)
    fresh = fresh_ref[...].astype(jnp.float32)
    lane = lax.broadcasted_iota(jnp.int32, (GROUP, page_len), 1)
    near_tops, near_totals, near_outs = [], [], []
    for first in range(0, slots, NEAR_BLOCK):
        block = range(first, first + NEAR_BLOCK)
        index = {}
        scores = {}
        for slot in block:
            for place in range(places):
                index[slot, place] = pages[slot, place]
            keys = [pool_ref[index[slot, place], :, :HEAD_DIM] for place in range(places)]
            score = SCALE * lax.dot_general(
                q_heads[slot].astype(jnp.bfloat16),
                jnp.concatenate(keys, 0),
                NT,
                preferred_element_type=jnp.float32,
            )
            scores[slot] = [
                jnp.where(
                    lane < limits[slot:slot + 1, at:at + 1],
                    score[:, at * page_len:(at + 1) * page_len],
                    NEVER,
                )
                for at in range(places)
            ]
        owns = [
            SCALE
            * jnp.sum(q_heads[slot] * fresh[slot:slot + 1, :HEAD_DIM], axis=1, keepdims=True)
            for slot in block
        ]
        tops = []
        for slot, own in zip(block, owns):
            top = scores[slot][0]
            for score in scores[slot][1:]:
                top = jnp.maximum(top, score)
            tops.append(jnp.maximum(jnp.max(top, axis=1, keepdims=True), own))
        weights = [jnp.exp(own - top) for own, top in zip(owns, tops)]
        for slot, top, weight in zip(block, tops, weights):
            probs = [jnp.exp(score - top).astype(jnp.bfloat16) for score in scores[slot]]
            summed = probs[0].astype(jnp.float32)
            for prob in probs[1:]:
                summed = summed + prob.astype(jnp.float32)
            values = [pool_ref[index[slot, place], :, HEAD_DIM:] for place in range(places)]
            out = jnp.dot(
                jnp.concatenate(probs, 1),
                jnp.concatenate(values, 0),
                preferred_element_type=jnp.float32,
            )
            total = jnp.sum(summed, axis=1, keepdims=True) + weight
            near_tops.append(top)
            near_totals.append(total)
            near_outs.append(out + weight * fresh[slot:slot + 1, HEAD_DIM:])
    return near_tops, near_totals, near_outs


def join_kernel(
    pages_ref, lengths_ref, q_ref, fresh_ref, pool_ref, back_ref, rows_ref, q_heads, heads
):
    near_tops, near_totals, near_outs = near_parts(
        pages_ref, lengths_ref, q_ref, fresh_ref, pool_ref, q_heads
    )
    slots = range(pages_ref.shape[0])
    places = range(FAR_POSITIONS)
    pages = pages_ref[...]
    senders = jnp.maximum(pages - POOL, 0)
    parts = [
        [back_ref[senders[slot, place]].astype(jnp.float32) for place in places]
        for slot in slots
    ]
    tops = [
        [
            jnp.where(
                pages[slot:slot + 1, place:place + 1] >= POOL,
                parts[slot][place][GROUP:, 0:1],
                NEVER,
            )
            for place in places
        ]
        for slot in slots
    ]
    totals = [[part[GROUP:, 1:2] + part[GROUP:, 2:3] for part in row] for row in parts]
    peaks = near_tops
    for place in places:
        peaks = [jnp.maximum(peak, row[place]) for peak, row in zip(peaks, tops)]
    keeps = [jnp.exp(top - peak) for top, peak in zip(near_tops, peaks)]
    denoms = [keep * total for total, keep in zip(near_totals, keeps)]
    numers = [keep * out for out, keep in zip(near_outs, keeps)]
    for place in places:
        for slot in slots:
            weight = jnp.exp(tops[slot][place] - peaks[slot]) * totals[slot][place]
            denoms[slot] = denoms[slot] + weight
            numers[slot] = numers[slot] + weight * parts[slot][place][:GROUP]
    for slot in slots:
        heads[slot] = numers[slot] / denoms[slot]
    for head in range(GROUP):
        block = heads[:, head, :].astype(jnp.bfloat16)
        for copy in range(rows_ref.shape[0]):
            rows_ref[copy, :, head * HEAD_DIM:(head + 1) * HEAD_DIM] = block


def project_kernel(rows_ref, which_ref, wo_ref, down_ref, up_ref, part_ref):
    rows = rows_ref[...]
    count = rows.shape[0]
    shrink = jnp.dot(rows, down_ref[...], preferred_element_type=jnp.float32)
    base = jnp.dot(rows, wo_ref[...], preferred_element_type=jnp.float32)
    adapter_of = lax.broadcasted_iota(jnp.int32, shrink.shape, 1) // ADAPTER_RANK
    which = down_rows(which_ref[...])
    shrink = jnp.where(which == adapter_of, shrink, 0.0)
    high = shrink.astype(jnp.bfloat16)
    low = (shrink - high.astype(jnp.float32)).astype(jnp.bfloat16)
    both = jnp.dot(
        jnp.concatenate([high, low], 0), up_ref[...], preferred_element_type=jnp.float32
    )
    part_ref[...] = (base + both[:count] + both[count:]).astype(jnp.bfloat16)


def body(
    queries,
    current_key_value,
    key_value_pages,
    transfer_pages,
    request_pages,
    lengths,
    request_adapter,
    residual_input,
    wo,
    down_weight,
    up_weight,
):
    slots, _ = request_pages.shape
    peers = transfer_pages.shape[1]
    heads = (slots, GROUP, HEAD_DIM)
    around = ("inst", "batch")
    params = pltpu.CompilerParams(vmem_limit_bytes=16 * 1024 * 1024)
    out_q = pl.pallas_call(
        outgoing_kernel,
        out_shape=jax.ShapeDtypeStruct((peers, GROUP, HEAD_DIM), jnp.bfloat16),
        in_specs=[HBM, HBM],
        out_specs=VMEM,
        scratch_shapes=[
            pltpu.VMEM(request_pages.shape, jnp.int32),
            pltpu.VMEM(queries.shape, jnp.bfloat16),
            pltpu.VMEM(heads, jnp.float32),
            pltpu.VMEM((peers + 1, GROUP, HEAD_DIM), jnp.float32),
            pltpu.SemaphoreType.DMA((2,)),
        ],
        compiler_params=params,
        cost_estimate=pl.CostEstimate(
            flops=100_000_000_000, bytes_accessed=400_000_000, transcendentals=0
        ),
        name="outgoing",
    )(in_hbm(request_pages), in_hbm(queries))
    in_q = lax.all_to_all(out_q, around, 0, 0, tiled=True)
    far = pl.pallas_call(
        far_kernel,
        out_shape=jax.ShapeDtypeStruct((peers, 2 * GROUP, HEAD_DIM), jnp.bfloat16),
        in_specs=[VMEM, VMEM, VMEM],
        out_specs=VMEM,
        compiler_params=params,
        cost_estimate=pl.CostEstimate(
            flops=100_000_000_000, bytes_accessed=400_000_000, transcendentals=0
        ),
        name="far",
    )(transfer_pages, in_q, key_value_pages)
    back = lax.all_to_all(far, around, 0, 0, tiled=True)
    group = lax.axis_size("batch")
    copies = pl.pallas_call(
        join_kernel,
        out_shape=jax.ShapeDtypeStruct((group, slots, GROUP * HEAD_DIM), jnp.bfloat16),
        in_specs=[VMEM] * 6,
        out_specs=VMEM,
        scratch_shapes=[pltpu.VMEM(heads, jnp.float32), pltpu.VMEM(heads, jnp.float32)],
        compiler_params=params,
        cost_estimate=pl.CostEstimate(
            flops=100_000_000_000, bytes_accessed=400_000_000, transcendentals=0
        ),
        name="join",
    )(
        request_pages,
        lengths[None],
        queries,
        current_key_value,
        key_value_pages,
        back,
    )
    rows = lax.all_to_all(copies, "batch", 0, 0, tiled=True).reshape(-1, GROUP * HEAD_DIM)
    part = pl.pallas_call(
        project_kernel,
        out_shape=jax.ShapeDtypeStruct((rows.shape[0], wo.shape[1]), jnp.bfloat16),
        in_specs=[VMEM] * 5,
        out_specs=VMEM,
        compiler_params=params,
        name="project",
    )(rows, request_adapter[None], wo, down_weight, up_weight)
    parts = lax.all_to_all(
        part.reshape(lax.axis_size("tensor"), -1, part.shape[1]), "tensor", 0, 0, tiled=True
    )
    summed = jnp.sum(parts.astype(jnp.float32), axis=0)
    return (residual_input.astype(jnp.float32) + summed).astype(jnp.bfloat16)


def solution(mesh):
    return jax.shard_map(
        body,
        mesh=mesh,
        in_specs=(
            P(("inst", "batch"), "tensor"),
            P(("inst", "batch"), "tensor"),
            P(("inst", "batch"), None, "tensor"),
            P(("inst", "batch"), None),
            P(("inst", "batch"), None),
            P(("inst", "batch")),
            P("inst"),
            P(("inst", "tensor"), "batch"),
            P("tensor", "batch"),
            P("tensor", None),
            P(None, "batch"),
        ),
        out_specs=P(("inst", "tensor"), "batch"),
        check_vma=False,
    )
```

```python
import math

import jax
import jax.numpy as jnp
from jax import lax
from jax.experimental import pallas as pl
from jax.experimental.pallas import tpu as pltpu
from jax.sharding import PartitionSpec as P

HEAD_DIM = 128
GROUP = 8
ADAPTER_RANK = 64
FAR_POSITIONS = 4
FAR_BLOCK = 32
NEAR_BLOCK = 8
POOL = 64
SCALE = 1.0 / math.sqrt(HEAD_DIM)
NEVER = -1e30
VMEM = pl.BlockSpec(memory_space=pltpu.VMEM)
NT = (((1,), (1,)), ((), ()))
AHEAD = pl.CostEstimate(flops=100_000_000_000, bytes_accessed=400_000_000, transcendentals=0)


def down_rows(line):
    square = (line.shape[1], line.shape[1])
    diagonal = lax.broadcasted_iota(jnp.int32, square, 0) == lax.broadcasted_iota(
        jnp.int32, square, 1
    )
    column = jnp.sum(jnp.where(diagonal, line.astype(jnp.float32), 0.0), axis=1, keepdims=True)
    return column.astype(jnp.int32)


def heads_of(q_ref, q_heads):
    q = q_ref[...].astype(jnp.float32)
    for head in range(GROUP):
        q_heads[:, head, :] = q[:, head * HEAD_DIM:(head + 1) * HEAD_DIM]


def opening_kernel(out_ref):
    out_ref[...] = jnp.zeros_like(out_ref)


def outgoing_kernel(opening_ref, pages_ref, q_ref, out_ref, q_heads, rows):
    rows[...] = opening_ref[...]
    heads_of(q_ref, q_heads)
    slots, peers = q_ref.shape[0], out_ref.shape[0]
    pages = pages_ref[...]
    targets = jnp.where(pages >= POOL, pages - POOL, peers)
    for slot in range(slots):
        for place in range(FAR_POSITIONS):
            rows[targets[slot, place]] = q_heads[slot]
    out_ref[...] = rows[:peers].astype(jnp.bfloat16)


def far_kernel(listed_ref, q_ref, pool_ref, out_ref):
    peers = q_ref.shape[0]
    page_len = pool_ref.shape[1]
    lane = lax.broadcasted_iota(jnp.int32, (GROUP, HEAD_DIM), 1)
    none = jnp.zeros((GROUP, page_len), jnp.bfloat16)
    listed = jnp.maximum(listed_ref[...], 0)
    for first in range(0, peers, FAR_BLOCK):
        block = range(first, first + FAR_BLOCK)
        pages = [listed[0, peer] for peer in block]
        scores = []
        for at in range(0, FAR_BLOCK, 2):
            peer = first + at
            keys = jnp.concatenate(
                [pool_ref[pages[at], :, :HEAD_DIM], pool_ref[pages[at + 1], :, :HEAD_DIM]], 0
            )
            both = jnp.concatenate([q_ref[peer], q_ref[peer + 1]], 0)
            score = SCALE * lax.dot_general(both, keys, NT, preferred_element_type=jnp.float32)
            scores += [score[:GROUP, :page_len], score[GROUP:, page_len:]]
        tops = [
            jnp.max(score, axis=1, keepdims=True).astype(jnp.bfloat16).astype(jnp.float32)
            for score in scores
        ]
        probs = [jnp.exp(score - top).astype(jnp.bfloat16) for score, top in zip(scores, tops)]
        totals = [jnp.sum(prob.astype(jnp.float32), axis=1, keepdims=True) for prob in probs]
        outs = []
        for at in range(0, FAR_BLOCK, 2):
            values = jnp.concatenate(
                [pool_ref[pages[at], :, HEAD_DIM:], pool_ref[pages[at + 1], :, HEAD_DIM:]], 0
            )
            both = jnp.concatenate(
                [
                    jnp.concatenate([probs[at], none], 1),
                    jnp.concatenate([none, probs[at + 1]], 1),
                ],
                0,
            )
            out = jnp.dot(both, values, preferred_element_type=jnp.float32)
            outs += [out[:GROUP], out[GROUP:]]
        for peer, out, top, total in zip(block, outs, tops, totals):
            high = total.astype(jnp.bfloat16).astype(jnp.float32)
            stats = jnp.where(lane == 0, top, jnp.where(lane == 1, high, total - high))
            out_ref[peer] = jnp.concatenate([out / total, stats], 0).astype(jnp.bfloat16)


def near_parts(pages_ref, lengths_ref, q_ref, fresh_ref, pool_ref, q_heads):
    slots, places = pages_ref.shape
    page_len = pool_ref.shape[1]
    pages = pages_ref[...]
    before = page_len * lax.broadcasted_iota(jnp.int32, pages.shape, 1)
    limits = jnp.where(pages < POOL, down_rows(lengths_ref[...]) - before, 0)
    pages = jnp.where(pages < POOL, pages, 0)
    heads_of(q_ref, q_heads)
    fresh = fresh_ref[...].astype(jnp.float32)
    lane = lax.broadcasted_iota(jnp.int32, (GROUP, page_len), 1)
    near_tops, near_totals, near_outs = [], [], []
    for first in range(0, slots, NEAR_BLOCK):
        block = range(first, first + NEAR_BLOCK)
        index = {}
        scores = {}
        for slot in block:
            for place in range(places):
                index[slot, place] = pages[slot, place]
            keys = [pool_ref[index[slot, place], :, :HEAD_DIM] for place in range(places)]
            score = SCALE * lax.dot_general(
                q_heads[slot].astype(jnp.bfloat16),
                jnp.concatenate(keys, 0),
                NT,
                preferred_element_type=jnp.float32,
            )
            scores[slot] = [
                jnp.where(
                    lane < limits[slot:slot + 1, at:at + 1],
                    score[:, at * page_len:(at + 1) * page_len],
                    NEVER,
                )
                for at in range(places)
            ]
        owns = [
            SCALE
            * jnp.sum(q_heads[slot] * fresh[slot:slot + 1, :HEAD_DIM], axis=1, keepdims=True)
            for slot in block
        ]
        tops = []
        for slot, own in zip(block, owns):
            top = scores[slot][0]
            for score in scores[slot][1:]:
                top = jnp.maximum(top, score)
            tops.append(jnp.maximum(jnp.max(top, axis=1, keepdims=True), own))
        weights = [jnp.exp(own - top) for own, top in zip(owns, tops)]
        for slot, top, weight in zip(block, tops, weights):
            probs = [jnp.exp(score - top).astype(jnp.bfloat16) for score in scores[slot]]
            summed = probs[0].astype(jnp.float32)
            for prob in probs[1:]:
                summed = summed + prob.astype(jnp.float32)
            values = [pool_ref[index[slot, place], :, HEAD_DIM:] for place in range(places)]
            out = jnp.dot(
                jnp.concatenate(probs, 1),
                jnp.concatenate(values, 0),
                preferred_element_type=jnp.float32,
            )
            total = jnp.sum(summed, axis=1, keepdims=True) + weight
            near_tops.append(top)
            near_totals.append(total)
            near_outs.append(out + weight * fresh[slot:slot + 1, HEAD_DIM:])
    return near_tops, near_totals, near_outs


def join_kernel(
    pages_ref, lengths_ref, q_ref, fresh_ref, pool_ref, back_ref, rows_ref, q_heads, heads
):
    near_tops, near_totals, near_outs = near_parts(
        pages_ref, lengths_ref, q_ref, fresh_ref, pool_ref, q_heads
    )
    slots = range(pages_ref.shape[0])
    places = range(FAR_POSITIONS)
    pages = pages_ref[...]
    senders = jnp.maximum(pages - POOL, 0)
    parts = [
        [back_ref[senders[slot, place]].astype(jnp.float32) for place in places]
        for slot in slots
    ]
    tops = [
        [
            jnp.where(
                pages[slot:slot + 1, place:place + 1] >= POOL,
                parts[slot][place][GROUP:, 0:1],
                NEVER,
            )
            for place in places
        ]
        for slot in slots
    ]
    totals = [[part[GROUP:, 1:2] + part[GROUP:, 2:3] for part in row] for row in parts]
    peaks = near_tops
    for place in places:
        peaks = [jnp.maximum(peak, row[place]) for peak, row in zip(peaks, tops)]
    keeps = [jnp.exp(top - peak) for top, peak in zip(near_tops, peaks)]
    denoms = [keep * total for total, keep in zip(near_totals, keeps)]
    numers = [keep * out for out, keep in zip(near_outs, keeps)]
    for place in places:
        for slot in slots:
            weight = jnp.exp(tops[slot][place] - peaks[slot]) * totals[slot][place]
            denoms[slot] = denoms[slot] + weight
            numers[slot] = numers[slot] + weight * parts[slot][place][:GROUP]
    for slot in slots:
        heads[slot] = numers[slot] / denoms[slot]
    for head in range(GROUP):
        block = heads[:, head, :].astype(jnp.bfloat16)
        for copy in range(rows_ref.shape[0]):
            rows_ref[copy, :, head * HEAD_DIM:(head + 1) * HEAD_DIM] = block


def project_kernel(rows_ref, which_ref, wo_ref, down_ref, up_ref, part_ref):
    rows = rows_ref[...]
    count = rows.shape[0]
    shrink = jnp.dot(rows, down_ref[...], preferred_element_type=jnp.float32)
    base = jnp.dot(rows, wo_ref[...], preferred_element_type=jnp.float32)
    adapter_of = lax.broadcasted_iota(jnp.int32, shrink.shape, 1) // ADAPTER_RANK
    which = down_rows(which_ref[...])
    shrink = jnp.where(which == adapter_of, shrink, 0.0)
    high = shrink.astype(jnp.bfloat16)
    low = (shrink - high.astype(jnp.float32)).astype(jnp.bfloat16)
    both = jnp.dot(
        jnp.concatenate([high, low], 0), up_ref[...], preferred_element_type=jnp.float32
    )
    part_ref[...] = (base + both[:count] + both[count:]).astype(jnp.bfloat16)


def body(
    queries,
    current_key_value,
    key_value_pages,
    transfer_pages,
    request_pages,
    lengths,
    request_adapter,
    residual_input,
    wo,
    down_weight,
    up_weight,
):
    slots, _ = request_pages.shape
    peers = transfer_pages.shape[1]
    heads = (slots, GROUP, HEAD_DIM)
    around = ("inst", "batch")
    params = pltpu.CompilerParams(vmem_limit_bytes=16 * 1024 * 1024)
    opening = pl.pallas_call(
        opening_kernel,
        out_shape=jax.ShapeDtypeStruct((peers + 1, GROUP, HEAD_DIM), jnp.float32),
        out_specs=VMEM,
        compiler_params=params,
        cost_estimate=AHEAD,
        name="opening",
    )()
    out_q = pl.pallas_call(
        outgoing_kernel,
        out_shape=jax.ShapeDtypeStruct((peers, GROUP, HEAD_DIM), jnp.bfloat16),
        in_specs=[VMEM] * 3,
        out_specs=VMEM,
        scratch_shapes=[
            pltpu.VMEM(heads, jnp.float32),
            pltpu.VMEM((peers + 1, GROUP, HEAD_DIM), jnp.float32),
        ],
        compiler_params=params,
        cost_estimate=AHEAD,
        name="outgoing",
    )(opening, request_pages, queries)
    in_q = lax.all_to_all(out_q, around, 0, 0, tiled=True)
    far = pl.pallas_call(
        far_kernel,
        out_shape=jax.ShapeDtypeStruct((peers, 2 * GROUP, HEAD_DIM), jnp.bfloat16),
        in_specs=[VMEM, VMEM, VMEM],
        out_specs=VMEM,
        compiler_params=params,
        cost_estimate=AHEAD,
        name="far",
    )(transfer_pages, in_q, key_value_pages)
    back = lax.all_to_all(far, around, 0, 0, tiled=True)
    group = lax.axis_size("batch")
    copies = pl.pallas_call(
        join_kernel,
        out_shape=jax.ShapeDtypeStruct((group, slots, GROUP * HEAD_DIM), jnp.bfloat16),
        in_specs=[VMEM] * 6,
        out_specs=VMEM,
        scratch_shapes=[pltpu.VMEM(heads, jnp.float32), pltpu.VMEM(heads, jnp.float32)],
        compiler_params=params,
        cost_estimate=AHEAD,
        name="join",
    )(
        request_pages,
        lengths[None],
        queries,
        current_key_value,
        key_value_pages,
        back,
    )
    rows = lax.all_to_all(copies, "batch", 0, 0, tiled=True).reshape(-1, GROUP * HEAD_DIM)
    part = pl.pallas_call(
        project_kernel,
        out_shape=jax.ShapeDtypeStruct((rows.shape[0], wo.shape[1]), jnp.bfloat16),
        in_specs=[VMEM] * 5,
        out_specs=VMEM,
        compiler_params=params,
        name="project",
    )(rows, request_adapter[None], wo, down_weight, up_weight)
    parts = lax.all_to_all(
        part.reshape(lax.axis_size("tensor"), -1, part.shape[1]), "tensor", 0, 0, tiled=True
    )
    summed = jnp.sum(parts.astype(jnp.float32), axis=0)
    return (residual_input.astype(jnp.float32) + summed).astype(jnp.bfloat16)


def solution(mesh):
    return jax.shard_map(
        body,
        mesh=mesh,
        in_specs=(
            P(("inst", "batch"), "tensor"),
            P(("inst", "batch"), "tensor"),
            P(("inst", "batch"), None, "tensor"),
            P(("inst", "batch"), None),
            P(("inst", "batch"), None),
            P(("inst", "batch")),
            P("inst"),
            P(("inst", "tensor"), "batch"),
            P("tensor", "batch"),
            P("tensor", None),
            P(None, "batch"),
        ),
        out_specs=P(("inst", "tensor"), "batch"),
        check_vma=False,
    )
```

```python
import math

import jax
import jax.numpy as jnp
from jax import lax
from jax.experimental import pallas as pl
from jax.experimental.pallas import tpu as pltpu
from jax.sharding import PartitionSpec as P

HEAD_DIM = 128
GROUP = 8
ADAPTER_RANK = 64
FAR_POSITIONS = 4
POOL = 64
SCALE = 1.0 / math.sqrt(HEAD_DIM)
NEVER = -1e30
VMEM = pl.BlockSpec(memory_space=pltpu.VMEM)
NT = (((1,), (1,)), ((), ()))
AHEAD = pl.CostEstimate(flops=100_000_000_000, bytes_accessed=400_000_000, transcendentals=0)


def down_rows(line):
    square = (line.shape[1], line.shape[1])
    diagonal = lax.broadcasted_iota(jnp.int32, square, 0) == lax.broadcasted_iota(
        jnp.int32, square, 1
    )
    column = jnp.sum(jnp.where(diagonal, line.astype(jnp.float32), 0.0), axis=1, keepdims=True)
    return column.astype(jnp.int32)


def heads_of(q_ref, q_heads):
    q = q_ref[...].astype(jnp.float32)
    for head in range(GROUP):
        q_heads[:, head, :] = q[:, head * HEAD_DIM:(head + 1) * HEAD_DIM]


def opening_kernel(out_ref):
    out_ref[...] = jnp.zeros_like(out_ref)


def outgoing_kernel(opening_ref, pages_ref, q_ref, out_ref, q_heads, rows):
    rows[...] = opening_ref[...]
    heads_of(q_ref, q_heads)
    slots, peers = q_ref.shape[0], out_ref.shape[0]
    pages = pages_ref[...]
    targets = jnp.where(pages >= POOL, pages - POOL, peers)
    for slot in range(slots):
        for place in range(FAR_POSITIONS):
            rows[targets[slot, place]] = q_heads[slot]
    out_ref[...] = rows[:peers].astype(jnp.bfloat16)


def attend_kernel(
    listed_ref, in_q_ref, pool_ref, pages_ref, lengths_ref, q_ref, fresh_ref,
    far_ref, near_ref, top_ref, total_ref, q_heads,
):
    peers = range(in_q_ref.shape[0])
    slots = range(pages_ref.shape[0])
    places = range(pages_ref.shape[1])
    page_len = pool_ref.shape[1]
    lane = lax.broadcasted_iota(jnp.int32, (GROUP, page_len), 1)
    none = jnp.zeros((GROUP, page_len), jnp.bfloat16)
    listed = jnp.maximum(listed_ref[...], 0)
    listed = [listed[0, peer] for peer in peers]
    pages = pages_ref[...]
    before = page_len * lax.broadcasted_iota(jnp.int32, pages.shape, 1)
    limits = jnp.where(pages < POOL, down_rows(lengths_ref[...]) - before, 0)
    pages = jnp.where(pages < POOL, pages, 0)
    index = [[pages[slot, place] for place in places] for slot in slots]
    heads_of(q_ref, q_heads)
    fresh = fresh_ref[...].astype(jnp.float32)

    far_scores, near_scores = [], []
    for peer in peers[::2]:
        keys = [pool_ref[listed[at], :, :HEAD_DIM] for at in (peer, peer + 1)]
        both = jnp.concatenate([in_q_ref[peer], in_q_ref[peer + 1]], 0)
        score = SCALE * lax.dot_general(
            both, jnp.concatenate(keys, 0), NT, preferred_element_type=jnp.float32
        )
        far_scores += [score[:GROUP, :page_len], score[GROUP:, page_len:]]
    for slot in slots:
        keys = [pool_ref[index[slot][place], :, :HEAD_DIM] for place in places]
        score = SCALE * lax.dot_general(
            q_heads[slot].astype(jnp.bfloat16),
            jnp.concatenate(keys, 0),
            NT,
            preferred_element_type=jnp.float32,
        )
        near_scores.append(
            [
                jnp.where(
                    lane < limits[slot:slot + 1, at:at + 1],
                    score[:, at * page_len:(at + 1) * page_len],
                    NEVER,
                )
                for at in places
            ]
        )

    far_tops = [
        jnp.max(score, axis=1, keepdims=True).astype(jnp.bfloat16).astype(jnp.float32)
        for score in far_scores
    ]
    owns = [
        SCALE * jnp.sum(q_heads[slot] * fresh[slot:slot + 1, :HEAD_DIM], axis=1, keepdims=True)
        for slot in slots
    ]
    near_tops = []
    for slot in slots:
        top = near_scores[slot][0]
        for score in near_scores[slot][1:]:
            top = jnp.maximum(top, score)
        near_tops.append(jnp.maximum(jnp.max(top, axis=1, keepdims=True), owns[slot]))
    far_probs = [
        jnp.exp(score - top).astype(jnp.bfloat16) for score, top in zip(far_scores, far_tops)
    ]
    far_totals = [
        jnp.sum(prob.astype(jnp.float32), axis=1, keepdims=True) for prob in far_probs
    ]
    near_probs = [
        [jnp.exp(score - top).astype(jnp.bfloat16) for score in row]
        for row, top in zip(near_scores, near_tops)
    ]
    weights = [jnp.exp(own - top) for own, top in zip(owns, near_tops)]

    far_outs = []
    for peer in peers[::2]:
        values = [pool_ref[listed[at], :, HEAD_DIM:] for at in (peer, peer + 1)]
        both = jnp.concatenate(
            [
                jnp.concatenate([far_probs[peer], none], 1),
                jnp.concatenate([none, far_probs[peer + 1]], 1),
            ],
            0,
        )
        out = jnp.dot(both, jnp.concatenate(values, 0), preferred_element_type=jnp.float32)
        far_outs += [out[:GROUP], out[GROUP:]]
    for slot in slots:
        values = [pool_ref[index[slot][place], :, HEAD_DIM:] for place in places]
        out = jnp.dot(
            jnp.concatenate(near_probs[slot], 1),
            jnp.concatenate(values, 0),
            preferred_element_type=jnp.float32,
        )
        summed = near_probs[slot][0].astype(jnp.float32)
        for prob in near_probs[slot][1:]:
            summed = summed + prob.astype(jnp.float32)
        total = jnp.sum(summed, axis=1, keepdims=True) + weights[slot]
        near_ref[slot] = out + weights[slot] * fresh[slot:slot + 1, HEAD_DIM:]
        top_ref[slot] = jnp.broadcast_to(near_tops[slot], out.shape)
        total_ref[slot] = jnp.broadcast_to(total, out.shape)
    for peer in peers:
        total = far_totals[peer]
        high = total.astype(jnp.bfloat16).astype(jnp.float32)
        stats = jnp.where(lane == 0, far_tops[peer], jnp.where(lane == 1, high, total - high))
        far_ref[peer] = jnp.concatenate([far_outs[peer] / total, stats], 0).astype(jnp.bfloat16)


def join_kernel(pages_ref, near_ref, top_ref, total_ref, back_ref, rows_ref, heads):
    slots = range(pages_ref.shape[0])
    places = range(FAR_POSITIONS)
    near_tops = [top_ref[slot] for slot in slots]
    near_totals = [total_ref[slot] for slot in slots]
    near_outs = [near_ref[slot] for slot in slots]
    pages = pages_ref[...]
    senders = jnp.maximum(pages - POOL, 0)
    parts = [
        [back_ref[senders[slot, place]].astype(jnp.float32) for place in places]
        for slot in slots
    ]
    tops = [
        [
            jnp.where(
                pages[slot:slot + 1, place:place + 1] >= POOL,
                parts[slot][place][GROUP:, 0:1],
                NEVER,
            )
            for place in places
        ]
        for slot in slots
    ]
    totals = [[part[GROUP:, 1:2] + part[GROUP:, 2:3] for part in row] for row in parts]
    peaks = near_tops
    for place in places:
        peaks = [jnp.maximum(peak, row[place]) for peak, row in zip(peaks, tops)]
    keeps = [jnp.exp(top - peak) for top, peak in zip(near_tops, peaks)]
    denoms = [keep * total for total, keep in zip(near_totals, keeps)]
    numers = [keep * out for out, keep in zip(near_outs, keeps)]
    for place in places:
        for slot in slots:
            weight = jnp.exp(tops[slot][place] - peaks[slot]) * totals[slot][place]
            denoms[slot] = denoms[slot] + weight
            numers[slot] = numers[slot] + weight * parts[slot][place][:GROUP]
    for slot in slots:
        heads[slot] = numers[slot] / denoms[slot]
    for head in range(GROUP):
        block = heads[:, head, :].astype(jnp.bfloat16)
        for copy in range(rows_ref.shape[0]):
            rows_ref[copy, :, head * HEAD_DIM:(head + 1) * HEAD_DIM] = block


def project_kernel(rows_ref, which_ref, wo_ref, down_ref, up_ref, part_ref):
    rows = rows_ref[...]
    count = rows.shape[0]
    shrink = jnp.dot(rows, down_ref[...], preferred_element_type=jnp.float32)
    base = jnp.dot(rows, wo_ref[...], preferred_element_type=jnp.float32)
    adapter_of = lax.broadcasted_iota(jnp.int32, shrink.shape, 1) // ADAPTER_RANK
    which = down_rows(which_ref[...])
    shrink = jnp.where(which == adapter_of, shrink, 0.0)
    high = shrink.astype(jnp.bfloat16)
    low = (shrink - high.astype(jnp.float32)).astype(jnp.bfloat16)
    both = jnp.dot(
        jnp.concatenate([high, low], 0), up_ref[...], preferred_element_type=jnp.float32
    )
    part_ref[...] = (base + both[:count] + both[count:]).astype(jnp.bfloat16)


def body(
    queries,
    current_key_value,
    key_value_pages,
    transfer_pages,
    request_pages,
    lengths,
    request_adapter,
    residual_input,
    wo,
    down_weight,
    up_weight,
):
    slots, _ = request_pages.shape
    peers = transfer_pages.shape[1]
    heads = (slots, GROUP, HEAD_DIM)
    around = ("inst", "batch")
    params = pltpu.CompilerParams(vmem_limit_bytes=16 * 1024 * 1024)
    opening = pl.pallas_call(
        opening_kernel,
        out_shape=jax.ShapeDtypeStruct((peers + 1, GROUP, HEAD_DIM), jnp.float32),
        out_specs=VMEM,
        compiler_params=params,
        cost_estimate=AHEAD,
        name="opening",
    )()
    out_q = pl.pallas_call(
        outgoing_kernel,
        out_shape=jax.ShapeDtypeStruct((peers, GROUP, HEAD_DIM), jnp.bfloat16),
        in_specs=[VMEM] * 3,
        out_specs=VMEM,
        scratch_shapes=[
            pltpu.VMEM(heads, jnp.float32),
            pltpu.VMEM((peers + 1, GROUP, HEAD_DIM), jnp.float32),
        ],
        compiler_params=params,
        cost_estimate=AHEAD,
        name="outgoing",
    )(opening, request_pages, queries)
    in_q = lax.all_to_all(out_q, around, 0, 0, tiled=True)
    far, near_out, near_top, near_total = pl.pallas_call(
        attend_kernel,
        out_shape=[jax.ShapeDtypeStruct((peers, 2 * GROUP, HEAD_DIM), jnp.bfloat16)]
        + [jax.ShapeDtypeStruct(heads, jnp.float32)] * 3,
        in_specs=[VMEM] * 7,
        out_specs=[VMEM] * 4,
        scratch_shapes=[pltpu.VMEM(heads, jnp.float32)],
        compiler_params=params,
        cost_estimate=AHEAD,
        name="attend",
    )(
        transfer_pages,
        in_q,
        key_value_pages,
        request_pages,
        lengths[None],
        queries,
        current_key_value,
    )
    back = lax.all_to_all(far, around, 0, 0, tiled=True)
    group = lax.axis_size("batch")
    copies = pl.pallas_call(
        join_kernel,
        out_shape=jax.ShapeDtypeStruct((group, slots, GROUP * HEAD_DIM), jnp.bfloat16),
        in_specs=[VMEM] * 5,
        out_specs=VMEM,
        scratch_shapes=[pltpu.VMEM(heads, jnp.float32)],
        compiler_params=params,
        cost_estimate=AHEAD,
        name="join",
    )(request_pages, near_out, near_top, near_total, back)
    rows = lax.all_to_all(copies, "batch", 0, 0, tiled=True).reshape(-1, GROUP * HEAD_DIM)
    part = pl.pallas_call(
        project_kernel,
        out_shape=jax.ShapeDtypeStruct((rows.shape[0], wo.shape[1]), jnp.bfloat16),
        in_specs=[VMEM] * 5,
        out_specs=VMEM,
        compiler_params=params,
        name="project",
    )(rows, request_adapter[None], wo, down_weight, up_weight)
    parts = lax.all_to_all(
        part.reshape(lax.axis_size("tensor"), -1, part.shape[1]), "tensor", 0, 0, tiled=True
    )
    summed = jnp.sum(parts.astype(jnp.float32), axis=0)
    return (residual_input.astype(jnp.float32) + summed).astype(jnp.bfloat16)


def solution(mesh):
    return jax.shard_map(
        body,
        mesh=mesh,
        in_specs=(
            P(("inst", "batch"), "tensor"),
            P(("inst", "batch"), "tensor"),
            P(("inst", "batch"), None, "tensor"),
            P(("inst", "batch"), None),
            P(("inst", "batch"), None),
            P(("inst", "batch")),
            P("inst"),
            P(("inst", "tensor"), "batch"),
            P("tensor", "batch"),
            P("tensor", None),
            P(None, "batch"),
        ),
        out_specs=P(("inst", "tensor"), "batch"),
        check_vma=False,
    )
```

```python
import math

import jax
import jax.numpy as jnp
from jax import lax
from jax.experimental import pallas as pl
from jax.experimental.pallas import tpu as pltpu
from jax.sharding import PartitionSpec as P

HEAD_DIM = 128
GROUP = 8
ADAPTER_RANK = 64
FAR_POSITIONS = 4
POOL = 64
SCALE = 1.0 / math.sqrt(HEAD_DIM)
NEVER = -1e30
VMEM = pl.BlockSpec(memory_space=pltpu.VMEM)
NT = (((1,), (1,)), ((), ()))
NOTHING = pl.CostEstimate(flops=0, bytes_accessed=0, transcendentals=0)
AHEAD = pl.CostEstimate(flops=100_000_000_000, bytes_accessed=400_000_000, transcendentals=0)


def down_rows(line):
    square = (line.shape[1], line.shape[1])
    diagonal = lax.broadcasted_iota(jnp.int32, square, 0) == lax.broadcasted_iota(
        jnp.int32, square, 1
    )
    column = jnp.sum(jnp.where(diagonal, line.astype(jnp.float32), 0.0), axis=1, keepdims=True)
    return column.astype(jnp.int32)


def heads_of(q_ref, q_heads):
    q = q_ref[...].astype(jnp.float32)
    for head in range(GROUP):
        q_heads[:, head, :] = q[:, head * HEAD_DIM:(head + 1) * HEAD_DIM]


def opening_kernel(out_ref):
    out_ref[...] = jnp.zeros_like(out_ref)


def outgoing_kernel(opening_ref, pages_ref, q_ref, out_ref, q_heads, rows):
    rows[...] = opening_ref[...]
    heads_of(q_ref, q_heads)
    slots, peers = q_ref.shape[0], out_ref.shape[0]
    pages = pages_ref[...]
    targets = jnp.where(pages >= POOL, pages - POOL, peers)
    for slot in range(slots):
        for place in range(FAR_POSITIONS):
            rows[targets[slot, place]] = q_heads[slot]
    out_ref[...] = rows[:peers].astype(jnp.bfloat16)


def attend_kernel(
    listed_ref, in_q_ref, pool_ref, pages_ref, lengths_ref, q_ref, fresh_ref,
    far_ref, near_ref, top_ref, total_ref, q_heads,
):
    peers = range(in_q_ref.shape[0])
    slots = range(pages_ref.shape[0])
    places = range(pages_ref.shape[1])
    page_len = pool_ref.shape[1]
    lane = lax.broadcasted_iota(jnp.int32, (GROUP, page_len), 1)
    none = jnp.zeros((GROUP, page_len), jnp.bfloat16)
    listed = jnp.maximum(listed_ref[...], 0)
    listed = [listed[0, peer] for peer in peers]
    pages = pages_ref[...]
    before = page_len * lax.broadcasted_iota(jnp.int32, pages.shape, 1)
    limits = jnp.where(pages < POOL, down_rows(lengths_ref[...]) - before, 0)
    pages = jnp.where(pages < POOL, pages, 0)
    index = [[pages[slot, place] for place in places] for slot in slots]
    heads_of(q_ref, q_heads)
    fresh = fresh_ref[...].astype(jnp.float32)

    far_scores, near_scores = [], []
    for peer in peers[::2]:
        keys = [pool_ref[listed[at], :, :HEAD_DIM] for at in (peer, peer + 1)]
        both = jnp.concatenate([in_q_ref[peer], in_q_ref[peer + 1]], 0)
        score = SCALE * lax.dot_general(
            both, jnp.concatenate(keys, 0), NT, preferred_element_type=jnp.float32
        )
        far_scores += [score[:GROUP, :page_len], score[GROUP:, page_len:]]
    for slot in slots:
        keys = [pool_ref[index[slot][place], :, :HEAD_DIM] for place in places]
        score = SCALE * lax.dot_general(
            q_heads[slot].astype(jnp.bfloat16),
            jnp.concatenate(keys, 0),
            NT,
            preferred_element_type=jnp.float32,
        )
        near_scores.append(
            [
                jnp.where(
                    lane < limits[slot:slot + 1, at:at + 1],
                    score[:, at * page_len:(at + 1) * page_len],
                    NEVER,
                )
                for at in places
            ]
        )

    far_tops = [
        jnp.max(score, axis=1, keepdims=True).astype(jnp.bfloat16).astype(jnp.float32)
        for score in far_scores
    ]
    owns = [
        SCALE * jnp.sum(q_heads[slot] * fresh[slot:slot + 1, :HEAD_DIM], axis=1, keepdims=True)
        for slot in slots
    ]
    near_tops = []
    for slot in slots:
        top = near_scores[slot][0]
        for score in near_scores[slot][1:]:
            top = jnp.maximum(top, score)
        near_tops.append(jnp.maximum(jnp.max(top, axis=1, keepdims=True), owns[slot]))
    far_probs = [
        jnp.exp(score - top).astype(jnp.bfloat16) for score, top in zip(far_scores, far_tops)
    ]
    far_totals = [
        jnp.sum(prob.astype(jnp.float32), axis=1, keepdims=True) for prob in far_probs
    ]
    near_probs = [
        [jnp.exp(score - top).astype(jnp.bfloat16) for score in row]
        for row, top in zip(near_scores, near_tops)
    ]
    weights = [jnp.exp(own - top) for own, top in zip(owns, near_tops)]

    far_outs = []
    for peer in peers[::2]:
        values = [pool_ref[listed[at], :, HEAD_DIM:] for at in (peer, peer + 1)]
        both = jnp.concatenate(
            [
                jnp.concatenate([far_probs[peer], none], 1),
                jnp.concatenate([none, far_probs[peer + 1]], 1),
            ],
            0,
        )
        out = jnp.dot(both, jnp.concatenate(values, 0), preferred_element_type=jnp.float32)
        far_outs += [out[:GROUP], out[GROUP:]]
    for slot in slots:
        values = [pool_ref[index[slot][place], :, HEAD_DIM:] for place in places]
        out = jnp.dot(
            jnp.concatenate(near_probs[slot], 1),
            jnp.concatenate(values, 0),
            preferred_element_type=jnp.float32,
        )
        summed = near_probs[slot][0].astype(jnp.float32)
        for prob in near_probs[slot][1:]:
            summed = summed + prob.astype(jnp.float32)
        total = jnp.sum(summed, axis=1, keepdims=True) + weights[slot]
        near_ref[slot] = out + weights[slot] * fresh[slot:slot + 1, HEAD_DIM:]
        top_ref[slot] = jnp.broadcast_to(near_tops[slot], out.shape)
        total_ref[slot] = jnp.broadcast_to(total, out.shape)
    for peer in peers:
        total = far_totals[peer]
        high = total.astype(jnp.bfloat16).astype(jnp.float32)
        stats = jnp.where(lane == 0, far_tops[peer], jnp.where(lane == 1, high, total - high))
        far_ref[peer] = jnp.concatenate([far_outs[peer] / total, stats], 0).astype(jnp.bfloat16)


def join_kernel(pages_ref, near_ref, top_ref, total_ref, back_ref, rows_ref, heads):
    slots = range(pages_ref.shape[0])
    places = range(FAR_POSITIONS)
    near_tops = [top_ref[slot] for slot in slots]
    near_totals = [total_ref[slot] for slot in slots]
    near_outs = [near_ref[slot] for slot in slots]
    pages = pages_ref[...]
    senders = jnp.maximum(pages - POOL, 0)
    parts = [
        [back_ref[senders[slot, place]].astype(jnp.float32) for place in places]
        for slot in slots
    ]
    tops = [
        [
            jnp.where(
                pages[slot:slot + 1, place:place + 1] >= POOL,
                parts[slot][place][GROUP:, 0:1],
                NEVER,
            )
            for place in places
        ]
        for slot in slots
    ]
    totals = [[part[GROUP:, 1:2] + part[GROUP:, 2:3] for part in row] for row in parts]
    peaks = near_tops
    for place in places:
        peaks = [jnp.maximum(peak, row[place]) for peak, row in zip(peaks, tops)]
    keeps = [jnp.exp(top - peak) for top, peak in zip(near_tops, peaks)]
    denoms = [keep * total for total, keep in zip(near_totals, keeps)]
    numers = [keep * out for out, keep in zip(near_outs, keeps)]
    for place in places:
        for slot in slots:
            weight = jnp.exp(tops[slot][place] - peaks[slot]) * totals[slot][place]
            denoms[slot] = denoms[slot] + weight
            numers[slot] = numers[slot] + weight * parts[slot][place][:GROUP]
    for slot in slots:
        heads[slot] = numers[slot] / denoms[slot]
    for head in range(GROUP):
        block = heads[:, head, :].astype(jnp.bfloat16)
        for copy in range(rows_ref.shape[0]):
            rows_ref[copy, :, head * HEAD_DIM:(head + 1) * HEAD_DIM] = block


def project_kernel(rows_ref, which_ref, wo_ref, down_ref, up_ref, part_ref):
    rows = rows_ref[...]
    count = rows.shape[0]
    shrink = jnp.dot(rows, down_ref[...], preferred_element_type=jnp.float32)
    base = jnp.dot(rows, wo_ref[...], preferred_element_type=jnp.float32)
    adapter_of = lax.broadcasted_iota(jnp.int32, shrink.shape, 1) // ADAPTER_RANK
    which = down_rows(which_ref[...])
    shrink = jnp.where(which == adapter_of, shrink, 0.0)
    high = shrink.astype(jnp.bfloat16)
    low = (shrink - high.astype(jnp.float32)).astype(jnp.bfloat16)
    both = jnp.dot(
        jnp.concatenate([high, low], 0), up_ref[...], preferred_element_type=jnp.float32
    )
    part_ref[...] = (base + both[:count] + both[count:]).astype(jnp.bfloat16)


def body(
    queries,
    current_key_value,
    key_value_pages,
    transfer_pages,
    request_pages,
    lengths,
    request_adapter,
    residual_input,
    wo,
    down_weight,
    up_weight,
):
    slots, _ = request_pages.shape
    peers = transfer_pages.shape[1]
    heads = (slots, GROUP, HEAD_DIM)
    around = ("inst", "batch")
    params = pltpu.CompilerParams(vmem_limit_bytes=16 * 1024 * 1024)
    opening = pl.pallas_call(
        opening_kernel,
        out_shape=jax.ShapeDtypeStruct((peers + 1, GROUP, HEAD_DIM), jnp.float32),
        out_specs=VMEM,
        compiler_params=params,
        cost_estimate=AHEAD,
        name="opening",
    )()
    out_q = pl.pallas_call(
        outgoing_kernel,
        out_shape=jax.ShapeDtypeStruct((peers, GROUP, HEAD_DIM), jnp.bfloat16),
        in_specs=[VMEM] * 3,
        out_specs=VMEM,
        scratch_shapes=[
            pltpu.VMEM(heads, jnp.float32),
            pltpu.VMEM((peers + 1, GROUP, HEAD_DIM), jnp.float32),
        ],
        compiler_params=params,
        cost_estimate=AHEAD,
        name="outgoing",
    )(opening, request_pages, queries)
    in_q = lax.all_to_all(out_q, around, 0, 0, tiled=True)
    far, near_out, near_top, near_total = pl.pallas_call(
        attend_kernel,
        out_shape=[jax.ShapeDtypeStruct((peers, 2 * GROUP, HEAD_DIM), jnp.bfloat16)]
        + [jax.ShapeDtypeStruct(heads, jnp.float32)] * 3,
        in_specs=[VMEM] * 7,
        out_specs=[VMEM] * 4,
        scratch_shapes=[pltpu.VMEM(heads, jnp.float32)],
        compiler_params=params,
        cost_estimate=AHEAD,
        name="attend",
    )(
        transfer_pages,
        in_q,
        key_value_pages,
        request_pages,
        lengths[None],
        queries,
        current_key_value,
    )
    back = lax.all_to_all(far, around, 0, 0, tiled=True)
    group = lax.axis_size("batch")
    copies = pl.pallas_call(
        join_kernel,
        out_shape=jax.ShapeDtypeStruct((group, slots, GROUP * HEAD_DIM), jnp.bfloat16),
        in_specs=[VMEM] * 5,
        out_specs=VMEM,
        scratch_shapes=[pltpu.VMEM(heads, jnp.float32)],
        compiler_params=params,
        cost_estimate=NOTHING,
        name="join",
    )(request_pages, near_out, near_top, near_total, back)
    rows = lax.all_to_all(copies, "batch", 0, 0, tiled=True).reshape(-1, GROUP * HEAD_DIM)
    part = pl.pallas_call(
        project_kernel,
        out_shape=jax.ShapeDtypeStruct((rows.shape[0], wo.shape[1]), jnp.bfloat16),
        in_specs=[VMEM] * 5,
        out_specs=VMEM,
        compiler_params=params,
        name="project",
    )(rows, request_adapter[None], wo, down_weight, up_weight)
    parts = lax.all_to_all(
        part.reshape(lax.axis_size("tensor"), -1, part.shape[1]), "tensor", 0, 0, tiled=True
    )
    summed = jnp.sum(parts.astype(jnp.float32), axis=0)
    return (residual_input.astype(jnp.float32) + summed).astype(jnp.bfloat16)


def solution(mesh):
    return jax.shard_map(
        body,
        mesh=mesh,
        in_specs=(
            P(("inst", "batch"), "tensor"),
            P(("inst", "batch"), "tensor"),
            P(("inst", "batch"), None, "tensor"),
            P(("inst", "batch"), None),
            P(("inst", "batch"), None),
            P(("inst", "batch")),
            P("inst"),
            P(("inst", "tensor"), "batch"),
            P("tensor", "batch"),
            P("tensor", None),
            P(None, "batch"),
        ),
        out_specs=P(("inst", "tensor"), "batch"),
        check_vma=False,
    )
```

```python
import math

import jax
import jax.numpy as jnp
from jax import lax
from jax.experimental import pallas as pl
from jax.experimental.pallas import tpu as pltpu
from jax.sharding import PartitionSpec as P

HEAD_DIM = 128
GROUP = 8
ADAPTER_RANK = 64
FAR_POSITIONS = 4
POOL = 64
SCALE = 1.0 / math.sqrt(HEAD_DIM)
NEVER = -1e30
VMEM = pl.BlockSpec(memory_space=pltpu.VMEM)
NT = (((1,), (1,)), ((), ()))
NOTHING = pl.CostEstimate(flops=0, bytes_accessed=0, transcendentals=0)
AHEAD = pl.CostEstimate(flops=100_000_000_000, bytes_accessed=400_000_000, transcendentals=0)


def down_rows(line):
    square = (line.shape[1], line.shape[1])
    diagonal = lax.broadcasted_iota(jnp.int32, square, 0) == lax.broadcasted_iota(
        jnp.int32, square, 1
    )
    column = jnp.sum(jnp.where(diagonal, line.astype(jnp.float32), 0.0), axis=1, keepdims=True)
    return column.astype(jnp.int32)


def heads_of(q_ref, q_heads):
    q = q_ref[...].astype(jnp.float32)
    for head in range(GROUP):
        q_heads[:, head, :] = q[:, head * HEAD_DIM:(head + 1) * HEAD_DIM]


def opening_kernel(out_ref):
    out_ref[...] = jnp.zeros_like(out_ref)


def outgoing_kernel(opening_ref, pages_ref, q_ref, out_ref, q_heads, rows):
    rows[...] = opening_ref[...]
    heads_of(q_ref, q_heads)
    slots, peers = q_ref.shape[0], out_ref.shape[0]
    pages = pages_ref[...]
    targets = jnp.where(pages >= POOL, pages - POOL, peers)
    for slot in range(slots):
        for place in range(FAR_POSITIONS):
            rows[targets[slot, place]] = q_heads[slot]
    out_ref[...] = rows[:peers].astype(jnp.bfloat16)


def attend_kernel(
    listed_ref, in_q_ref, pool_ref, pages_ref, lengths_ref, q_ref, fresh_ref,
    far_ref, near_ref, top_ref, total_ref, q_heads,
):
    peers = range(in_q_ref.shape[0])
    slots = range(pages_ref.shape[0])
    places = range(pages_ref.shape[1])
    page_len = pool_ref.shape[1]
    lane = lax.broadcasted_iota(jnp.int32, (GROUP, page_len), 1)
    none = jnp.zeros((GROUP, page_len), jnp.bfloat16)
    listed = jnp.maximum(listed_ref[...], 0)
    listed = [listed[0, peer] for peer in peers]
    pages = pages_ref[...]
    before = page_len * lax.broadcasted_iota(jnp.int32, pages.shape, 1)
    limits = jnp.where(pages < POOL, down_rows(lengths_ref[...]) - before, 0)
    pages = jnp.where(pages < POOL, pages, 0)
    index = [[pages[slot, place] for place in places] for slot in slots]
    heads_of(q_ref, q_heads)
    fresh = fresh_ref[...].astype(jnp.float32)

    far_scores, near_scores = [], []
    for peer in peers[::2]:
        keys = [pool_ref[listed[at], :, :HEAD_DIM] for at in (peer, peer + 1)]
        both = jnp.concatenate([in_q_ref[peer], in_q_ref[peer + 1]], 0)
        score = SCALE * lax.dot_general(
            both, jnp.concatenate(keys, 0), NT, preferred_element_type=jnp.float32
        )
        far_scores += [score[:GROUP, :page_len], score[GROUP:, page_len:]]
    for slot in slots:
        keys = [pool_ref[index[slot][place], :, :HEAD_DIM] for place in places]
        score = SCALE * lax.dot_general(
            q_heads[slot].astype(jnp.bfloat16),
            jnp.concatenate(keys, 0),
            NT,
            preferred_element_type=jnp.float32,
        )
        near_scores.append(
            [
                jnp.where(
                    lane < limits[slot:slot + 1, at:at + 1],
                    score[:, at * page_len:(at + 1) * page_len],
                    NEVER,
                )
                for at in places
            ]
        )

    far_tops = [
        jnp.max(score, axis=1, keepdims=True).astype(jnp.bfloat16).astype(jnp.float32)
        for score in far_scores
    ]
    owns = [
        SCALE * jnp.sum(q_heads[slot] * fresh[slot:slot + 1, :HEAD_DIM], axis=1, keepdims=True)
        for slot in slots
    ]
    near_tops = []
    for slot in slots:
        top = near_scores[slot][0]
        for score in near_scores[slot][1:]:
            top = jnp.maximum(top, score)
        near_tops.append(jnp.maximum(jnp.max(top, axis=1, keepdims=True), owns[slot]))
    far_probs = [
        jnp.exp(score - top).astype(jnp.bfloat16) for score, top in zip(far_scores, far_tops)
    ]
    far_totals = [
        jnp.sum(prob.astype(jnp.float32), axis=1, keepdims=True) for prob in far_probs
    ]
    near_probs = [
        [jnp.exp(score - top).astype(jnp.bfloat16) for score in row]
        for row, top in zip(near_scores, near_tops)
    ]
    weights = [jnp.exp(own - top) for own, top in zip(owns, near_tops)]

    far_outs = []
    for peer in peers[::2]:
        values = [pool_ref[listed[at], :, HEAD_DIM:] for at in (peer, peer + 1)]
        both = jnp.concatenate(
            [
                jnp.concatenate([far_probs[peer], none], 1),
                jnp.concatenate([none, far_probs[peer + 1]], 1),
            ],
            0,
        )
        out = jnp.dot(both, jnp.concatenate(values, 0), preferred_element_type=jnp.float32)
        far_outs += [out[:GROUP], out[GROUP:]]
    for slot in slots:
        values = [pool_ref[index[slot][place], :, HEAD_DIM:] for place in places]
        out = jnp.dot(
            jnp.concatenate(near_probs[slot], 1),
            jnp.concatenate(values, 0),
            preferred_element_type=jnp.float32,
        )
        summed = near_probs[slot][0].astype(jnp.float32)
        for prob in near_probs[slot][1:]:
            summed = summed + prob.astype(jnp.float32)
        total = jnp.sum(summed, axis=1, keepdims=True) + weights[slot]
        near_ref[slot] = out + weights[slot] * fresh[slot:slot + 1, HEAD_DIM:]
        top_ref[slot] = jnp.broadcast_to(near_tops[slot], out.shape)
        total_ref[slot] = jnp.broadcast_to(total, out.shape)
    for peer in peers:
        total = far_totals[peer]
        high = total.astype(jnp.bfloat16).astype(jnp.float32)
        stats = jnp.where(lane == 0, far_tops[peer], jnp.where(lane == 1, high, total - high))
        far_ref[peer] = jnp.concatenate([far_outs[peer] / total, stats], 0).astype(jnp.bfloat16)


def join_kernel(pages_ref, near_ref, top_ref, total_ref, back_ref, rows_ref, heads):
    slots = range(pages_ref.shape[0])
    places = range(FAR_POSITIONS)
    near_tops = [top_ref[slot] for slot in slots]
    near_totals = [total_ref[slot] for slot in slots]
    near_outs = [near_ref[slot] for slot in slots]
    pages = pages_ref[...]
    senders = jnp.maximum(pages - POOL, 0)
    parts = [
        [back_ref[senders[slot, place]].astype(jnp.float32) for place in places]
        for slot in slots
    ]
    tops = [
        [
            jnp.where(
                pages[slot:slot + 1, place:place + 1] >= POOL,
                parts[slot][place][GROUP:, 0:1],
                NEVER,
            )
            for place in places
        ]
        for slot in slots
    ]
    totals = [[part[GROUP:, 1:2] + part[GROUP:, 2:3] for part in row] for row in parts]
    peaks = near_tops
    for place in places:
        peaks = [jnp.maximum(peak, row[place]) for peak, row in zip(peaks, tops)]
    keeps = [jnp.exp(top - peak) for top, peak in zip(near_tops, peaks)]
    denoms = [keep * total for total, keep in zip(near_totals, keeps)]
    numers = [keep * out for out, keep in zip(near_outs, keeps)]
    for place in places:
        for slot in slots:
            weight = jnp.exp(tops[slot][place] - peaks[slot]) * totals[slot][place]
            denoms[slot] = denoms[slot] + weight
            numers[slot] = numers[slot] + weight * parts[slot][place][:GROUP]
    for slot in slots:
        heads[slot] = numers[slot] / denoms[slot]
    for head in range(GROUP):
        block = heads[:, head, :].astype(jnp.bfloat16)
        for copy in range(rows_ref.shape[0]):
            rows_ref[copy, :, head * HEAD_DIM:(head + 1) * HEAD_DIM] = block


def project_kernel(rows_ref, which_ref, wo_ref, down_ref, up_ref, part_ref):
    rows = rows_ref[...]
    count = rows.shape[0]
    shrink = jnp.dot(rows, down_ref[...], preferred_element_type=jnp.float32)
    base = jnp.dot(rows, wo_ref[...], preferred_element_type=jnp.float32)
    adapter_of = lax.broadcasted_iota(jnp.int32, shrink.shape, 1) // ADAPTER_RANK
    which = down_rows(which_ref[...])
    shrink = jnp.where(which == adapter_of, shrink, 0.0)
    high = shrink.astype(jnp.bfloat16)
    low = (shrink - high.astype(jnp.float32)).astype(jnp.bfloat16)
    both = jnp.dot(
        jnp.concatenate([high, low], 0), up_ref[...], preferred_element_type=jnp.float32
    )
    part_ref[...] = (base + both[:count] + both[count:]).astype(jnp.bfloat16)


def body(
    queries,
    current_key_value,
    key_value_pages,
    transfer_pages,
    request_pages,
    lengths,
    request_adapter,
    residual_input,
    wo,
    down_weight,
    up_weight,
):
    slots, _ = request_pages.shape
    peers = transfer_pages.shape[1]
    heads = (slots, GROUP, HEAD_DIM)
    around = ("inst", "batch")
    params = pltpu.CompilerParams(vmem_limit_bytes=16 * 1024 * 1024)
    opening = pl.pallas_call(
        opening_kernel,
        out_shape=jax.ShapeDtypeStruct((peers + 1, GROUP, HEAD_DIM), jnp.float32),
        out_specs=VMEM,
        compiler_params=params,
        cost_estimate=AHEAD,
        name="opening",
    )()
    out_q = pl.pallas_call(
        outgoing_kernel,
        out_shape=jax.ShapeDtypeStruct((peers, GROUP, HEAD_DIM), jnp.bfloat16),
        in_specs=[VMEM] * 3,
        out_specs=VMEM,
        scratch_shapes=[
            pltpu.VMEM(heads, jnp.float32),
            pltpu.VMEM((peers + 1, GROUP, HEAD_DIM), jnp.float32),
        ],
        compiler_params=params,
        cost_estimate=AHEAD,
        name="outgoing",
    )(opening, request_pages, queries)
    in_q = lax.all_to_all(out_q, around, 0, 0, tiled=True)
    far, near_out, near_top, near_total = pl.pallas_call(
        attend_kernel,
        out_shape=[jax.ShapeDtypeStruct((peers, 2 * GROUP, HEAD_DIM), jnp.bfloat16)]
        + [jax.ShapeDtypeStruct(heads, jnp.float32)] * 3,
        in_specs=[VMEM] * 7,
        out_specs=[VMEM] * 4,
        scratch_shapes=[pltpu.VMEM(heads, jnp.float32)],
        compiler_params=params,
        cost_estimate=NOTHING,
        name="attend",
    )(
        transfer_pages,
        in_q,
        key_value_pages,
        request_pages,
        lengths[None],
        queries,
        current_key_value,
    )
    back = lax.all_to_all(far, around, 0, 0, tiled=True)
    group = lax.axis_size("batch")
    copies = pl.pallas_call(
        join_kernel,
        out_shape=jax.ShapeDtypeStruct((group, slots, GROUP * HEAD_DIM), jnp.bfloat16),
        in_specs=[VMEM] * 5,
        out_specs=VMEM,
        scratch_shapes=[pltpu.VMEM(heads, jnp.float32)],
        compiler_params=params,
        cost_estimate=NOTHING,
        name="join",
    )(request_pages, near_out, near_top, near_total, back)
    rows = lax.all_to_all(copies, "batch", 0, 0, tiled=True).reshape(-1, GROUP * HEAD_DIM)
    part = pl.pallas_call(
        project_kernel,
        out_shape=jax.ShapeDtypeStruct((rows.shape[0], wo.shape[1]), jnp.bfloat16),
        in_specs=[VMEM] * 5,
        out_specs=VMEM,
        compiler_params=params,
        name="project",
    )(rows, request_adapter[None], wo, down_weight, up_weight)
    parts = lax.all_to_all(
        part.reshape(lax.axis_size("tensor"), -1, part.shape[1]), "tensor", 0, 0, tiled=True
    )
    summed = jnp.sum(parts.astype(jnp.float32), axis=0)
    return (residual_input.astype(jnp.float32) + summed).astype(jnp.bfloat16)


def solution(mesh):
    return jax.shard_map(
        body,
        mesh=mesh,
        in_specs=(
            P(("inst", "batch"), "tensor"),
            P(("inst", "batch"), "tensor"),
            P(("inst", "batch"), None, "tensor"),
            P(("inst", "batch"), None),
            P(("inst", "batch"), None),
            P(("inst", "batch")),
            P("inst"),
            P(("inst", "tensor"), "batch"),
            P("tensor", "batch"),
            P("tensor", None),
            P(None, "batch"),
        ),
        out_specs=P(("inst", "tensor"), "batch"),
        check_vma=False,
    )
```

```python
import math

import jax
import jax.numpy as jnp
from jax import lax
from jax.experimental import pallas as pl
from jax.experimental.pallas import tpu as pltpu
from jax.sharding import PartitionSpec as P

HEAD_DIM = 128
GROUP = 8
ADAPTER_RANK = 64
FAR_POSITIONS = 4
FAR_BLOCK = 32
NEAR_BLOCK = 8
POOL = 64
SCALE = 1.0 / math.sqrt(HEAD_DIM)
NEVER = -1e30
VMEM = pl.BlockSpec(memory_space=pltpu.VMEM)
NT = (((1,), (1,)), ((), ()))
NOTHING = pl.CostEstimate(flops=0, bytes_accessed=0, transcendentals=0)
AHEAD = pl.CostEstimate(flops=100_000_000_000, bytes_accessed=400_000_000, transcendentals=0)


def down_rows(line):
    square = (line.shape[1], line.shape[1])
    diagonal = lax.broadcasted_iota(jnp.int32, square, 0) == lax.broadcasted_iota(
        jnp.int32, square, 1
    )
    column = jnp.sum(jnp.where(diagonal, line.astype(jnp.float32), 0.0), axis=1, keepdims=True)
    return column.astype(jnp.int32)


def heads_of(q_ref, q_heads):
    q = q_ref[...].astype(jnp.float32)
    for head in range(GROUP):
        q_heads[:, head, :] = q[:, head * HEAD_DIM:(head + 1) * HEAD_DIM]


def opening_kernel(out_ref):
    out_ref[...] = jnp.zeros_like(out_ref)


def outgoing_kernel(opening_ref, pages_ref, q_ref, out_ref, q_heads, rows):
    rows[...] = opening_ref[...]
    heads_of(q_ref, q_heads)
    slots, peers = q_ref.shape[0], out_ref.shape[0]
    pages = pages_ref[...]
    targets = jnp.where(pages >= POOL, pages - POOL, peers)
    for slot in range(slots):
        for place in range(FAR_POSITIONS):
            rows[targets[slot, place]] = q_heads[slot]
    out_ref[...] = rows[:peers].astype(jnp.bfloat16)


def far_kernel(listed_ref, q_ref, pool_ref, out_ref):
    peers = q_ref.shape[0]
    page_len = pool_ref.shape[1]
    lane = lax.broadcasted_iota(jnp.int32, (GROUP, HEAD_DIM), 1)
    none = jnp.zeros((GROUP, page_len), jnp.bfloat16)
    listed = jnp.maximum(listed_ref[...], 0)
    for first in range(0, peers, FAR_BLOCK):
        block = range(first, first + FAR_BLOCK)
        pages = [listed[0, peer] for peer in block]
        scores = []
        for at in range(0, FAR_BLOCK, 2):
            peer = first + at
            keys = jnp.concatenate(
                [pool_ref[pages[at], :, :HEAD_DIM], pool_ref[pages[at + 1], :, :HEAD_DIM]], 0
            )
            both = jnp.concatenate([q_ref[peer], q_ref[peer + 1]], 0)
            score = SCALE * lax.dot_general(both, keys, NT, preferred_element_type=jnp.float32)
            scores += [score[:GROUP, :page_len], score[GROUP:, page_len:]]
        tops = [
            jnp.max(score, axis=1, keepdims=True).astype(jnp.bfloat16).astype(jnp.float32)
            for score in scores
        ]
        probs = [jnp.exp(score - top).astype(jnp.bfloat16) for score, top in zip(scores, tops)]
        totals = [jnp.sum(prob.astype(jnp.float32), axis=1, keepdims=True) for prob in probs]
        outs = []
        for at in range(0, FAR_BLOCK, 2):
            values = jnp.concatenate(
                [pool_ref[pages[at], :, HEAD_DIM:], pool_ref[pages[at + 1], :, HEAD_DIM:]], 0
            )
            both = jnp.concatenate(
                [
                    jnp.concatenate([probs[at], none], 1),
                    jnp.concatenate([none, probs[at + 1]], 1),
                ],
                0,
            )
            out = jnp.dot(both, values, preferred_element_type=jnp.float32)
            outs += [out[:GROUP], out[GROUP:]]
        for peer, out, top, total in zip(block, outs, tops, totals):
            high = total.astype(jnp.bfloat16).astype(jnp.float32)
            stats = jnp.where(lane == 0, top, jnp.where(lane == 1, high, total - high))
            out_ref[peer] = jnp.concatenate([out / total, stats], 0).astype(jnp.bfloat16)


def near_parts(pages_ref, lengths_ref, q_ref, fresh_ref, pool_ref, q_heads):
    slots, places = pages_ref.shape
    page_len = pool_ref.shape[1]
    pages = pages_ref[...]
    before = page_len * lax.broadcasted_iota(jnp.int32, pages.shape, 1)
    limits = jnp.where(pages < POOL, down_rows(lengths_ref[...]) - before, 0)
    pages = jnp.where(pages < POOL, pages, 0)
    heads_of(q_ref, q_heads)
    fresh = fresh_ref[...].astype(jnp.float32)
    lane = lax.broadcasted_iota(jnp.int32, (GROUP, page_len), 1)
    near_tops, near_totals, near_outs = [], [], []
    for first in range(0, slots, NEAR_BLOCK):
        block = range(first, first + NEAR_BLOCK)
        index = {}
        scores = {}
        for slot in block:
            for place in range(places):
                index[slot, place] = pages[slot, place]
            keys = [pool_ref[index[slot, place], :, :HEAD_DIM] for place in range(places)]
            score = SCALE * lax.dot_general(
                q_heads[slot].astype(jnp.bfloat16),
                jnp.concatenate(keys, 0),
                NT,
                preferred_element_type=jnp.float32,
            )
            scores[slot] = [
                jnp.where(
                    lane < limits[slot:slot + 1, at:at + 1],
                    score[:, at * page_len:(at + 1) * page_len],
                    NEVER,
                )
                for at in range(places)
            ]
        owns = [
            SCALE
            * jnp.sum(q_heads[slot] * fresh[slot:slot + 1, :HEAD_DIM], axis=1, keepdims=True)
            for slot in block
        ]
        tops = []
        for slot, own in zip(block, owns):
            top = scores[slot][0]
            for score in scores[slot][1:]:
                top = jnp.maximum(top, score)
            tops.append(jnp.maximum(jnp.max(top, axis=1, keepdims=True), own))
        weights = [jnp.exp(own - top) for own, top in zip(owns, tops)]
        for slot, top, weight in zip(block, tops, weights):
            probs = [jnp.exp(score - top).astype(jnp.bfloat16) for score in scores[slot]]
            summed = probs[0].astype(jnp.float32)
            for prob in probs[1:]:
                summed = summed + prob.astype(jnp.float32)
            values = [pool_ref[index[slot, place], :, HEAD_DIM:] for place in range(places)]
            out = jnp.dot(
                jnp.concatenate(probs, 1),
                jnp.concatenate(values, 0),
                preferred_element_type=jnp.float32,
            )
            total = jnp.sum(summed, axis=1, keepdims=True) + weight
            near_tops.append(top)
            near_totals.append(total)
            near_outs.append(out + weight * fresh[slot:slot + 1, HEAD_DIM:])
    return near_tops, near_totals, near_outs


def join_kernel(
    pages_ref, lengths_ref, q_ref, fresh_ref, pool_ref, back_ref, rows_ref, q_heads, heads
):
    near_tops, near_totals, near_outs = near_parts(
        pages_ref, lengths_ref, q_ref, fresh_ref, pool_ref, q_heads
    )
    slots = range(pages_ref.shape[0])
    places = range(FAR_POSITIONS)
    pages = pages_ref[...]
    senders = jnp.maximum(pages - POOL, 0)
    parts = [
        [back_ref[senders[slot, place]].astype(jnp.float32) for place in places]
        for slot in slots
    ]
    tops = [
        [
            jnp.where(
                pages[slot:slot + 1, place:place + 1] >= POOL,
                parts[slot][place][GROUP:, 0:1],
                NEVER,
            )
            for place in places
        ]
        for slot in slots
    ]
    totals = [[part[GROUP:, 1:2] + part[GROUP:, 2:3] for part in row] for row in parts]
    peaks = near_tops
    for place in places:
        peaks = [jnp.maximum(peak, row[place]) for peak, row in zip(peaks, tops)]
    keeps = [jnp.exp(top - peak) for top, peak in zip(near_tops, peaks)]
    denoms = [keep * total for total, keep in zip(near_totals, keeps)]
    numers = [keep * out for out, keep in zip(near_outs, keeps)]
    for place in places:
        for slot in slots:
            weight = jnp.exp(tops[slot][place] - peaks[slot]) * totals[slot][place]
            denoms[slot] = denoms[slot] + weight
            numers[slot] = numers[slot] + weight * parts[slot][place][:GROUP]
    for slot in slots:
        heads[slot] = numers[slot] / denoms[slot]
    for head in range(GROUP):
        block = heads[:, head, :].astype(jnp.bfloat16)
        for copy in range(rows_ref.shape[0]):
            rows_ref[copy, :, head * HEAD_DIM:(head + 1) * HEAD_DIM] = block


def project_kernel(rows_ref, which_ref, wo_ref, down_ref, up_ref, part_ref):
    rows = rows_ref[...]
    count = rows.shape[0]
    shrink = jnp.dot(rows, down_ref[...], preferred_element_type=jnp.float32)
    base = jnp.dot(rows, wo_ref[...], preferred_element_type=jnp.float32)
    adapter_of = lax.broadcasted_iota(jnp.int32, shrink.shape, 1) // ADAPTER_RANK
    which = down_rows(which_ref[...])
    shrink = jnp.where(which == adapter_of, shrink, 0.0)
    high = shrink.astype(jnp.bfloat16)
    low = (shrink - high.astype(jnp.float32)).astype(jnp.bfloat16)
    both = jnp.dot(
        jnp.concatenate([high, low], 0), up_ref[...], preferred_element_type=jnp.float32
    )
    part_ref[...] = (base + both[:count] + both[count:]).astype(jnp.bfloat16)


def body(
    queries,
    current_key_value,
    key_value_pages,
    transfer_pages,
    request_pages,
    lengths,
    request_adapter,
    residual_input,
    wo,
    down_weight,
    up_weight,
):
    slots, _ = request_pages.shape
    peers = transfer_pages.shape[1]
    heads = (slots, GROUP, HEAD_DIM)
    around = ("inst", "batch")
    params = pltpu.CompilerParams(vmem_limit_bytes=16 * 1024 * 1024)
    opening = pl.pallas_call(
        opening_kernel,
        out_shape=jax.ShapeDtypeStruct((peers + 1, GROUP, HEAD_DIM), jnp.float32),
        out_specs=VMEM,
        compiler_params=params,
        cost_estimate=AHEAD,
        name="opening",
    )()
    out_q = pl.pallas_call(
        outgoing_kernel,
        out_shape=jax.ShapeDtypeStruct((peers, GROUP, HEAD_DIM), jnp.bfloat16),
        in_specs=[VMEM] * 3,
        out_specs=VMEM,
        scratch_shapes=[
            pltpu.VMEM(heads, jnp.float32),
            pltpu.VMEM((peers + 1, GROUP, HEAD_DIM), jnp.float32),
        ],
        compiler_params=params,
        cost_estimate=AHEAD,
        name="outgoing",
    )(opening, request_pages, queries)
    in_q = lax.all_to_all(out_q, around, 0, 0, tiled=True)
    far = pl.pallas_call(
        far_kernel,
        out_shape=jax.ShapeDtypeStruct((peers, 2 * GROUP, HEAD_DIM), jnp.bfloat16),
        in_specs=[VMEM, VMEM, VMEM],
        out_specs=VMEM,
        compiler_params=params,
        cost_estimate=NOTHING,
        name="far",
    )(transfer_pages, in_q, key_value_pages)
    back = lax.all_to_all(far, around, 0, 0, tiled=True)
    group = lax.axis_size("batch")
    copies = pl.pallas_call(
        join_kernel,
        out_shape=jax.ShapeDtypeStruct((group, slots, GROUP * HEAD_DIM), jnp.bfloat16),
        in_specs=[VMEM] * 6,
        out_specs=VMEM,
        scratch_shapes=[pltpu.VMEM(heads, jnp.float32), pltpu.VMEM(heads, jnp.float32)],
        compiler_params=params,
        cost_estimate=NOTHING,
        name="join",
    )(
        request_pages,
        lengths[None],
        queries,
        current_key_value,
        key_value_pages,
        back,
    )
    rows = lax.all_to_all(copies, "batch", 0, 0, tiled=True).reshape(-1, GROUP * HEAD_DIM)
    part = pl.pallas_call(
        project_kernel,
        out_shape=jax.ShapeDtypeStruct((rows.shape[0], wo.shape[1]), jnp.bfloat16),
        in_specs=[VMEM] * 5,
        out_specs=VMEM,
        compiler_params=params,
        name="project",
    )(rows, request_adapter[None], wo, down_weight, up_weight)
    parts = lax.all_to_all(
        part.reshape(lax.axis_size("tensor"), -1, part.shape[1]), "tensor", 0, 0, tiled=True
    )
    summed = jnp.sum(parts.astype(jnp.float32), axis=0)
    return (residual_input.astype(jnp.float32) + summed).astype(jnp.bfloat16)


def solution(mesh):
    return jax.shard_map(
        body,
        mesh=mesh,
        in_specs=(
            P(("inst", "batch"), "tensor"),
            P(("inst", "batch"), "tensor"),
            P(("inst", "batch"), None, "tensor"),
            P(("inst", "batch"), None),
            P(("inst", "batch"), None),
            P(("inst", "batch")),
            P("inst"),
            P(("inst", "tensor"), "batch"),
            P("tensor", "batch"),
            P("tensor", None),
            P(None, "batch"),
        ),
        out_specs=P(("inst", "tensor"), "batch"),
        check_vma=False,
    )
```
